128 devices in a mesh: sec: 2 (over x_hi), lat: 4 (over y), lon: 16 (over z, x_lo, core).
Axes of the slice: x: 4 (x_hi: 2, x_lo: 2; x = x_hi * 2 + x_lo), y: 4, z: 4, core: 2. Of those that a mesh axis runs over, the one named last changes fastest.
Arguments:
- atmos: bfloat16 [256, 1440, 512], P(('sec', 'lat'), 'lon'), may hold values from -6 to 6
- ocean: bfloat16 [256, 1440, 384], P(('sec', 'lat'), 'lon'), may hold values from -6 to 6
- remap: int32 [256, 1440], P(('sec', 'lat'), 'lon'), may hold values from 0 to 368639, as said below
- fold: int32 [1440], P('lon'), may hold values from 0 to 1439, as said below
- sea_mask: int32 [256, 1440], P(('sec', 'lat'), 'lon'), may hold values 0 or 1
- flux_weight: bfloat16 [512, 384], replicated, may hold values from -0.25 to 0.25
- dw_kernel: float32 [2, 7, 7, 384], replicated, may hold values from -0.875 to 0.875
- norm_gain: float32 [2, 384], replicated, may hold values from 0.25 to 1.75
- w_in: bfloat16 [2, 384, 1536], replicated, may hold values from -0.3125 to 0.3125
- w_out: bfloat16 [2, 1536, 384], replicated, may hold values from -0.15625 to 0.15625
Outputs:
- ocean_next: bfloat16 [256, 1440, 384], P(('sec', 'lat'), 'lon')
The draws below stay inside these ranges and needn't reach their ends.
Inputs may be any that keep to these rules, and one draw needn't show every extreme that they name: For the ocean cell at row r and column c, remap holds s * 1440 + t where s // 32 == r // 32 and t = (c + d) mod 1440 with -45 <= d <= 45; both d = 45 and d = -45 occur. fold[c] = (p - 1 - c) mod 1440 for one p shared by all columns.
All inputs are finite; a program needn't handle non-finite values. No bound on the sum of `sea_mask` on one device may be relied on, other than what follows from the above.
Results may differ from the reference program's by a relative error of at most 0.014.
Values may be sent and summed in bfloat16 or wider, within the bound.
A program may use at most 128 MiB of HBM per device.

```python
import jax
import jax.numpy as jnp
from jax import lax

CA = 512
CO = 384
FF = 1536
KW = 7
BLOCKS = 2
ROWS = 32
REACH = 45
NLAT = 256
NLON = 1440


def draw_remap(key, part):
    key = jax.random.fold_in(key, 11)
    key_row, key_offset, key_pick = jax.random.split(key, 3)
    lat_index = jnp.arange(NLAT, dtype=jnp.int32)[:, None]
    lon_index = jnp.arange(NLON, dtype=jnp.int32)[None, :]
    src_row = lat_index // ROWS * ROWS + jax.random.randint(key_row, (NLAT, NLON), 0, ROWS, dtype=jnp.int32)
    offset = jax.random.randint(key_offset, (NLAT, NLON), -REACH, REACH + 1, dtype=jnp.int32)
    picker = jax.random.randint(key_pick, (NLAT, NLON), 0, 16, dtype=jnp.int32)
    offset = jnp.where(picker == 0, REACH, jnp.where(picker == 1, -REACH, offset))
    first_row = lat_index == 0
    offset = jnp.where(first_row & (lon_index == 1), REACH, offset)
    offset = jnp.where(first_row & (lon_index == 2), -REACH, offset)
    corner = first_row & (lon_index == 0) | (lat_index == NLAT - 1) & (lon_index == NLON - 1)
    src_row = jnp.where(corner, lat_index, src_row)
    offset = jnp.where(corner, 0, offset)
    return (src_row * NLON + (lon_index + offset) % NLON).astype(jnp.int32)


def draw_fold(key, part):
    key = jax.random.fold_in(key, 12)
    pivot = jax.random.randint(key, (), 0, NLON, dtype=jnp.int32)
    return ((pivot - 1 - jnp.arange(NLON, dtype=jnp.int32)) % NLON).astype(jnp.int32)


def touch_ends(result, key, smallest, high):
    longest = result.shape.index(max(result.shape))
    spots = []
    for shift in (0, 1):
        where = [jax.random.randint(jax.random.fold_in(key, axis), (), 0, length) for axis, length in enumerate(result.shape)]
        where[longest] = (where[longest] + shift) % result.shape[longest]
        spots.append(tuple(where))
    return result.at[spots[0]].set(smallest).at[spots[1]].set(high)


def block_scale(stream_key, shape, pieces, least, largest):
    loudness, own = 1.0, jax.random.fold_in(stream_key, 6)
    for dim, shards_of in pieces:
        steps = jnp.exp(jax.random.uniform(jax.random.fold_in(own, dim), (shards_of,), jnp.float32, least / len(pieces), largest / len(pieces)))
        loudness = loudness * jnp.repeat(steps, shape[dim] // shards_of).reshape([-1 if axis == dim else 1 for axis in range(len(shape))])
    return loudness


def centred(own_key, shape, width, limit, pieces=(), kind=jnp.bfloat16):
    level = block_scale(own_key, shape, pieces, -0.22, 0.18) if pieces else 1.0
    drawn = jax.random.normal(own_key, shape, jnp.float32) * width * level
    return jnp.minimum(jnp.maximum(drawn, -limit), limit).astype(kind)


def setup_inputs(seed: int = 0) -> dict:
    key_list = jax.random.split(jax.random.key(seed), 11)
    atmos = centred(key_list[0], (NLAT, NLON, CA), 1.0, 6.0, ((0, 8), (1, 16)))
    ocean = centred(key_list[1], (NLAT, NLON, CO), 1.0, 6.0, ((0, 8), (1, 16)))
    remap = draw_remap(jax.random.fold_in(key_list[10], 71), 0)
    fold = draw_fold(jax.random.fold_in(key_list[10], 71), 0)
    sea_mask = touch_ends((jax.random.randint(key_list[4], (NLAT, NLON), 0, 4) < 3).astype(jnp.int32), jax.random.fold_in(key_list[4], 1), 0, 1)
    flux_weight = centred(key_list[5], (CA, CO), CA ** -0.5, 0.25)
    dw_kernel = centred(key_list[6], (BLOCKS, KW, KW, CO), (KW * KW) ** -0.5, 0.875, (), jnp.float32)
    norm_gain = jnp.clip(1.0 + 0.15 * jax.random.normal(key_list[7], (BLOCKS, CO), jnp.float32), 0.25, 1.75)
    w_in = centred(key_list[8], (BLOCKS, CO, FF), CO ** -0.5, 0.3125)
    w_out = centred(key_list[9], (BLOCKS, FF, CO), FF ** -0.5, 0.15625)
    return dict(atmos=atmos, ocean=ocean, remap=remap, fold=fold, sea_mask=sea_mask, flux_weight=flux_weight, dw_kernel=dw_kernel, norm_gain=norm_gain, w_in=w_in, w_out=w_out)


def conv_block(state, sea_share, fold, kernel, gain, expand, contract):
    half = KW // 2
    masked = (sea_share * state).astype(jnp.bfloat16)
    north_rows = masked[NLAT - half:][::-1][:, fold]
    south_rows = jnp.zeros((half, NLON, CO), jnp.bfloat16)
    tall = jnp.concatenate([south_rows, masked, north_rows], axis=0)
    padded = jnp.concatenate([tall[:, NLON - half:], tall, tall[:, :half]], axis=1)
    conv = jnp.zeros((NLAT, NLON, CO), jnp.float32)
    for tap_row in range(KW):
        for tap_col in range(KW):
            conv = conv + padded[tap_row:tap_row + NLAT, tap_col:tap_col + NLON].astype(jnp.float32) * kernel[tap_row, tap_col]
    centre = lax.optimization_barrier(jnp.mean(conv, axis=-1, keepdims=True))
    spread = lax.optimization_barrier(jnp.mean((conv - centre) ** 2, axis=-1, keepdims=True))
    normed = ((conv - centre) * lax.rsqrt(spread + 1e-06) * gain).astype(jnp.bfloat16)

    def mlp_rows(block_rows):
        hidden = jax.nn.gelu(jnp.dot(block_rows, expand, preferred_element_type=jnp.float32)).astype(jnp.bfloat16)
        return jnp.dot(hidden, contract, preferred_element_type=jnp.float32)
    update = lax.map(mlp_rows, normed.reshape(-1, ROWS * NLON, CO)).reshape(NLAT, NLON, CO)
    return state + sea_share * update

def reference(atmos, ocean, remap, fold, sea_mask, flux_weight, dw_kernel, norm_gain, w_in, w_out):
    flux = jnp.dot(atmos.reshape(-1, CA), flux_weight, preferred_element_type=jnp.float32).astype(jnp.bfloat16)
    taken = jnp.take(flux, remap.reshape(-1), axis=0).reshape(NLAT, NLON, CO)
    sea_share = sea_mask.astype(jnp.float32)[..., None]
    state = ocean.astype(jnp.float32) + sea_share * taken.astype(jnp.float32)
    for block_index in range(BLOCKS):
        state = conv_block(state, sea_share, fold, dw_kernel[block_index], norm_gain[block_index], w_in[block_index], w_out[block_index])
    return state.astype(jnp.bfloat16)
```

```python
import functools

import jax
import jax.numpy as jnp
from jax import lax
from jax.experimental import pallas as pl
from jax.experimental.pallas import tpu as pltpu
from jax.sharding import PartitionSpec as P

ROWS, COLS, CH, CA, FF = 32, 90, 384, 512, 1536
HALF = 45
CELLS = ROWS * HALF
BANDS, LONS = 8, 16
NLON = COLS * LONS
NR, NT, NM, USED = 16, 48, 768, 720
QR, QT = 24, 50
LOW = ((0, 0), (1, 0), (0, 1))
ROW_HIGH = ((1, 14), (0, 15), (1, 15))
COL_HIGH = ((1, 43), (0, 44), (1, 44))
ROW_TOP = ((1, 17), (0, 18), (1, 18))
COL_TOP = ((1, 46), (0, 47), (1, 47))
MESH = pl.DeviceIdType.MESH
F32, BF16 = jnp.float32, jnp.bfloat16
VLIMIT = 60 * 2**20


def lane_low(shape):
    return lax.broadcasted_iota(jnp.int32, shape, len(shape) - 1) < 64


def strips(state, share, row_strip, col_strip, corner, tmp):
    for k in range(3):
        lanes = slice(k * 128, (k + 1) * 128)
        for side, edge in enumerate((LOW, ROW_HIGH)):
            for n, (a, big) in enumerate(edge):
                for b in range(2):
                    at = pl.ds(big, NT, stride=NR)
                    row_strip[side, n, b, :, lanes] = (
                        state[k, 2 * a + b, at, :] * share[2 * a + b, at, :]
                    ).astype(BF16)
        for side, edge in enumerate((LOW, COL_HIGH)):
            for n, (b, big) in enumerate(edge):
                for a in range(2):
                    at = slice(big * NR, (big + 1) * NR)
                    col_strip[side, n, a, :, lanes] = (
                        state[k, 2 * a + b, at, :] * share[2 * a + b, at, :]
                    ).astype(BF16)
        for rside, redge in enumerate((LOW, ROW_HIGH)):
            for cside, cedge in enumerate((LOW, COL_HIGH)):
                for n, (a, rbig) in enumerate(redge):
                    for m, (b, cbig) in enumerate(cedge):
                        at = slice(cbig * NR + rbig, cbig * NR + rbig + 1)
                        tmp[3 * n + m : 3 * n + m + 1, :] = (
                            state[k, 2 * a + b, at, :] * share[2 * a + b, at, :]
                        )
                corner[rside, cside, :, lanes] = tmp[0:16, :].astype(BF16)


def flux_kernel(
    picks, sea, atmos, ocean, weight,
    state, share, row_strip, col_strip, corner,
    table, outgoing, incoming, taken, tmp, send_sem, recv_sem,
):
    sec, lat, lon = (lax.axis_index(n) for n in ("sec", "lat", "lon"))
    left, right = lax.rem(lon + LONS - 1, LONS), lax.rem(lon + 1, LONS)
    barrier = pltpu.get_barrier_semaphore()
    for other in (left, right):
        pl.semaphore_signal(barrier, inc=1, device_id=(sec, lat, other), device_id_type=MESH)
    pl.semaphore_wait(barrier, 2)

    def copy(k, side):
        return pltpu.make_async_remote_copy(
            src_ref=outgoing.at[k, side],
            dst_ref=incoming.at[k, 1 - side],
            send_sem=send_sem.at[k, side],
            recv_sem=recv_sem.at[k, 1 - side],
            device_id=(sec, lat, (left, right)[side]),
            device_id_type=MESH,
        )

    for k in range(3):
        for side in range(2):

            def cells(i, _, k=k, side=side):
                at = pl.multiple_of(i * 288, 288)
                value = jnp.dot(
                    atmos[pl.ds(side * CELLS + at, 288), :],
                    weight[:, k * 128 : (k + 1) * 128],
                    preferred_element_type=F32,
                ).astype(BF16)
                outgoing[k, side, pl.ds(at, 288), :] = value
                table[k, pl.ds((1 + side) * CELLS + at, 288), :] = value.astype(F32)
                return 0

            lax.fori_loop(0, CELLS // 288, cells, 0)
            copy(k, side).start()
        table[k, 4 * CELLS : 4 * CELLS + 8, :] = jnp.zeros((8, 128), F32)

    tail = slice(USED, NM)
    for q in range(4):
        share[q, tail, :] = jnp.zeros((NM - USED, 128), F32)
        for k in range(3):
            state[k, q, tail, :] = jnp.zeros((NM - USED, 128), F32)
    tmp[...] = jnp.zeros_like(tmp)

    def ocean_cells(big, _):
        at = pl.ds(pl.multiple_of(big * NR, NR), NR)
        for b in range(2):
            for k in range(3):
                tmp[0:ROWS, :] = ocean[2 * big + b, :, k * 128 : (k + 1) * 128].astype(F32)
                for a in range(2):
                    state[k, 2 * a + b, at, :] = tmp[pl.ds(a, NR, stride=2), :]
        return 0

    lax.fori_loop(0, HALF, ocean_cells, 0)
    tmp[0:1, :] = jnp.zeros((1, 128), F32)
    tmp[1:2, :] = jnp.ones((1, 128), F32)

    def share_cells(big, _):
        base = pl.multiple_of(big * NR, NR)
        for a in range(2):
            for b in range(2):
                for r in range(NR):
                    share[2 * a + b, pl.ds(base + r, 1), :] = tmp[
                        pl.ds(sea[2 * r + a, 2 * big + b], 1), :
                    ]
        return 0

    lax.fori_loop(0, HALF, share_cells, 0)

    for k in range(3):
        for side in range(2):
            copy(k, 1 - side).wait_recv()

            def widened(i, _, k=k, side=side):
                at = pl.multiple_of(i * 288, 288)
                table[k, pl.ds(3 * side * CELLS + at, 288), :] = incoming[
                    k, side, pl.ds(at, 288), :
                ].astype(F32)
                return 0

            lax.fori_loop(0, CELLS // 288, widened, 0)

        def gather_cells(big, _, k=k):
            base = pl.multiple_of(big * NR, NR)
            for a in range(2):
                for b in range(2):
                    for r in range(NR):
                        taken[2 * a + b, pl.ds(base + r, 1), :] = table[
                            k, pl.ds(picks[2 * r + a, 2 * big + b], 1), :
                        ]
            return 0

        lax.fori_loop(0, HALF, gather_cells, 0)
        for q in range(4):
            state[k, q, 0:USED, :] += taken[q, 0:USED, :]
    strips(state, share, row_strip, col_strip, corner, tmp)
    for k in range(3):
        for side in range(2):
            copy(k, side).wait_send()


def halo_kernel(
    fold, row_strip, col_strip, corner,
    row_halo, col_halo, corner_halo, fold_halo,
    ring, send_sem, recv_sem, ring_send, ring_recv,
):
    sec, lat, lon = (lax.axis_index(n) for n in ("sec", "lat", "lon"))
    band = sec * 4 + lat
    left, right = lax.rem(lon + LONS - 1, LONS), lax.rem(lon + 1, LONS)
    has_north, has_south, top = band < BANDS - 1, band > 0, band == BANDS - 1

    def place(step, where):
        other = band + step
        return (other // 4, lax.rem(other, 4), where)

    def peer(step):
        return (sec, lat, lax.rem(lon + step, LONS))

    barrier = pltpu.get_barrier_semaphore()

    def greet(device):
        pl.semaphore_signal(barrier, inc=1, device_id=device, device_id_type=MESH)

    greet((sec, lat, left))
    greet((sec, lat, right))
    pl.when(has_north)(lambda: [greet(place(1, w)) for w in (left, lon, right)] and None)
    pl.when(has_south)(lambda: [greet(place(-1, w)) for w in (left, lon, right)] and None)
    pl.when(top)(lambda: [greet(peer(s)) for s in range(2, LONS - 1)] and None)
    greeted = 2 + jnp.where(has_north, 3, 0) + jnp.where(has_south, 3, 0) + jnp.where(top, LONS - 3, 0)
    pl.semaphore_wait(barrier, greeted)

    def copy(n, src, dst, device):
        return pltpu.make_async_remote_copy(
            src_ref=src, dst_ref=dst, send_sem=send_sem.at[n], recv_sem=recv_sem.at[n],
            device_id=device, device_id_type=MESH,
        )

    def sideways():
        return [
            copy(0, col_strip.at[1], col_halo.at[0], (sec, lat, right)),
            copy(1, col_strip.at[0], col_halo.at[1], (sec, lat, left)),
        ]

    def up():
        return [
            copy(2, row_strip.at[1], row_halo.at[0], place(1, lon)),
            copy(3, corner.at[1, 0], corner_halo.at[0, 1], place(1, left)),
            copy(4, corner.at[1, 1], corner_halo.at[0, 0], place(1, right)),
        ]

    def down():
        return [
            copy(5, row_strip.at[0], row_halo.at[1], place(-1, lon)),
            copy(6, corner.at[0, 0], corner_halo.at[1, 1], place(-1, left)),
            copy(7, corner.at[0, 1], corner_halo.at[1, 0], place(-1, right)),
        ]

    def ring_copy(step):
        return pltpu.make_async_remote_copy(
            src_ref=row_strip.at[1], dst_ref=ring.at[lon],
            send_sem=ring_send.at[step], recv_sem=ring_recv.at[step],
            device_id=peer(step), device_id_type=MESH,
        )

    def start(copies):
        for c in copies:
            c.start()

    pl.when(top)(lambda: start([ring_copy(s) for s in (8, 7, 9, 6, 10, 5, 11, 4, 12, 3, 13, 2, 14, 1, 15)]))
    pl.when(has_north)(lambda: start(up()))
    pl.when(has_south)(lambda: start(down()))
    start(sideways())

    @pl.when(jnp.logical_not(top))
    def _():
        fold_halo[...] = jnp.zeros_like(fold_halo)

    @pl.when(jnp.logical_not(has_south))
    def _():
        row_halo[0] = jnp.zeros(row_halo.shape[1:], BF16)
        corner_halo[0] = jnp.zeros(corner_halo.shape[1:], BF16)

    @pl.when(top)
    def _():
        row_halo[1] = jnp.zeros(row_halo.shape[1:], BF16)
        corner_halo[1] = jnp.zeros(corner_halo.shape[1:], BF16)
        ring[lon] = row_strip[1]
        for s in range(1, LONS):
            ring_copy(s).wait()
        first = lax.rem(fold[0] - 92 + NLON, NLON)
        sector = lax.div(first, COLS)
        off = first - sector * COLS
        out = lax.broadcasted_iota(jnp.int32, (2 * NT, 6 * NT), 0)
        k = lax.broadcasted_iota(jnp.int32, (2 * NT, 6 * NT), 1)
        high = out >= NT
        wanted = off + 95 - jnp.where(high, 2 * (out - NT) + 1, 2 * out)
        part = jnp.where(k >= 4 * NT, 2, jnp.where(k >= 2 * NT, 1, 0))
        inner = k - part * 2 * NT
        odd = inner >= NT
        pair = jnp.where(odd, inner - NT, inner)
        at = part * COLS + 2 * pair + jnp.where(odd, 1, 0)
        pick = jnp.where((at == wanted) & (pair < HALF), 1.0, 0.0).astype(BF16)
        parts = [ring[lax.rem(sector + s, LONS)] for s in range(3)]
        for n in range(3):
            got = jnp.zeros((2 * NT, CH), F32)
            for s in range(3):
                got += jnp.dot(
                    pick[:, s * 2 * NT : (s + 1) * 2 * NT],
                    parts[s][2 - n].reshape(2 * NT, CH),
                    preferred_element_type=F32,
                )
            fold_halo[n] = got.reshape(2, NT, CH).astype(BF16)

    def finish(outs, ins):
        for c in outs:
            c.wait_send()
        for c in ins:
            c.wait_recv()

    finish(sideways(), sideways())
    pl.when(has_north)(lambda: finish(up(), down()))
    pl.when(has_south)(lambda: finish(down(), up()))


def block_kernel(
    index, last, state_in, share, row_halo, col_halo, corner_halo, fold_halo, kernel_taps, gain, expand_all, contract_all, *rest
):
    *rest, padded, paired, lhs, rhs, conv, tmp, taps, expand, contract, load_sem = rest
    if last:
        out, state = rest
    else:
        state, row_strip, col_strip, corner = rest
    loads = [
        pltpu.make_async_copy(expand_all.at[index], expand, load_sem.at[0]),
        pltpu.make_async_copy(contract_all.at[index], contract, load_sem.at[1]),
    ]
    for load in loads:
        load.start()
    top = (lax.axis_index("sec") * 4 + lax.axis_index("lat")) == BANDS - 1
    padded[...] = jnp.zeros_like(padded)
    taps[...] = jnp.zeros_like(taps)
    tmp[0:16, :] = jnp.zeros((16, 128), F32)
    low8 = lane_low((8, 128))
    for row in range(7):
        for k in range(3):
            tmp[1:8, :] = kernel_taps[index, row, :, k * 128 : (k + 1) * 128]
            now, before = tmp[1:9, :], tmp[0:8, :]
            at = slice(8 * (row + 1), 8 * (row + 2))
            taps[2 * k, at, :] = jnp.where(low8, now, pltpu.roll(before, 64, 1))
            taps[2 * k + 1, at, :] = jnp.where(low8, pltpu.roll(now, 64, 1), before)

    for k in range(3):
        lanes = slice(k * 128, (k + 1) * 128)

        def own(big, _, k=k):
            src = pl.ds(pl.multiple_of(big * NR, NR), NR)
            for a in range(2):
                for b in range(2):
                    value = state_in[k, 2 * a + b, src, :] * share[2 * a + b, src, :]
                    padded[2 * (1 - a) + 1 - b, pl.ds((big + 1 + b) * QR + 1 + a, NR), :] = value
            return 0

        lax.fori_loop(0, HALF, own, 0)
        for side, places in enumerate((LOW, ROW_TOP)):
            for n, (pa, pr) in enumerate(places):
                for b in range(2):
                    padded[2 * pa + 1 - b, pl.ds((1 + b) * QR + pr, NT, stride=QR), :] = row_halo[
                        side, n, b, :, lanes
                    ].astype(F32)
        for side, places in enumerate((LOW, COL_TOP)):
            for n, (pb, pt) in enumerate(places):
                for a in range(2):
                    at = pt * QR + 1 + a
                    padded[2 * (1 - a) + pb, at : at + NR, :] = col_halo[
                        side, n, a, :, lanes
                    ].astype(F32)
        for rside, rplaces in enumerate((LOW, ROW_TOP)):
            for cside, cplaces in enumerate((LOW, COL_TOP)):
                tmp[0:16, :] = corner_halo[rside, cside, :, lanes].astype(F32)
                for n, (pa, pr) in enumerate(rplaces):
                    for m, (pb, pt) in enumerate(cplaces):
                        at = pt * QR + pr
                        padded[2 * pa + pb, at : at + 1, :] = tmp[3 * n + m : 3 * n + m + 1, :]

        @pl.when(top)
        def _(lanes=lanes):
            for n, (pa, pr) in enumerate(ROW_TOP):
                for pb in range(2):
                    padded[2 * pa + pb, pl.ds(pr, NT, stride=QR), :] = fold_halo[
                        n, pb, :, lanes
                    ].astype(F32)

        def pair_up(big, _):
            at = pl.ds(pl.multiple_of(big * QR, QR), QR)
            low = lane_low((QR, 128))
            for pa in range(2):
                even, odd = padded[2 * pa, at, :], padded[2 * pa + 1, at, :]
                paired[0, pa, at, :] = jnp.where(low, even, pltpu.roll(odd, 64, 1))
                paired[1, pa, at, :] = jnp.where(low, pltpu.roll(even, 64, 1), odd)
            return 0

        lax.fori_loop(0, NT, pair_up, 0)

        def spread(big, _):
            to = pl.ds(pl.multiple_of(big * NR, NR), NR)
            for g in range(2):
                for d in range(4):
                    for pa in range(2):
                        c0 = d * 256 + pa * 128
                        lhs[g, to, c0 : c0 + 128] = paired[
                            g, pa, pl.ds(big * QR + d, NR), :
                        ].astype(BF16)
            return 0

        lax.fori_loop(0, NT, spread, 0)

        def weights(i, _, k=k):
            dr, dt = i // 4, lax.rem(i, 4)
            diag = (
                lax.broadcasted_iota(jnp.int32, (64, 128), 0)
                == lax.broadcasted_iota(jnp.int32, (64, 128), 1) % 64
            )
            for g in range(2):
                for pa in range(2):
                    for pb in range(2):
                        to = pl.ds(pl.multiple_of(dr * 256 + pa * 128 + pb * 64, 64), 64)
                        for r in range(2):
                            at = (2 * dr + pa + 1 - r) * 8 + 2 * dt + pb
                            value = jnp.where(diag, taps[2 * k + g, pl.ds(at, 1), :], 0.0)
                            rhs[g, dt, to, r * 128 : (r + 1) * 128] = value.astype(BF16)
            return 0

        lax.fori_loop(0, 16, weights, 0)
        for g in range(2):

            def multiply(i, _, k=k, g=g):
                at = pl.multiple_of(i * 240, 240)
                total = None
                for d in range(4):
                    part = jnp.dot(
                        lhs[g, pl.ds(at + d * NR, 240), :], rhs[g, d], preferred_element_type=F32
                    )
                    total = part if total is None else total + part
                conv[2 * k + g, pl.ds(at, 240), :] = total
                return 0

            lax.fori_loop(0, USED // 240, multiply, 0)

    for load in loads:
        load.wait()
    tile = 240
    for a in range(2):

        def mlp(i, _, a=a):
            at = pl.ds(pl.multiple_of(i * tile, tile), tile)
            low = lane_low((tile, 128))
            chunks = []
            for k in range(3):
                even = conv[2 * k, at, a * 128 : (a + 1) * 128]
                odd = conv[2 * k + 1, at, a * 128 : (a + 1) * 128]
                chunks.append(
                    jnp.concatenate(
                        [
                            jnp.where(low, even, pltpu.roll(odd, 64, 1)),
                            jnp.where(low, pltpu.roll(even, 64, 1), odd),
                        ],
                        axis=0,
                    )
                )
            centre = jnp.sum(chunks[0] + chunks[1] + chunks[2], axis=1, keepdims=True) * (1.0 / CH)
            chunks = [c - centre for c in chunks]
            squares = chunks[0] * chunks[0] + chunks[1] * chunks[1] + chunks[2] * chunks[2]
            scale = lax.rsqrt(jnp.sum(squares, axis=1, keepdims=True) * (1.0 / CH) + 1e-06)
            normed = jnp.concatenate(
                [
                    (c * scale * gain[index, :, k * 128 : (k + 1) * 128]).astype(BF16)
                    for k, c in enumerate(chunks)
                ],
                axis=1,
            )
            update = None
            for f in range(0, FF, 512):
                u = jnp.dot(normed, expand[:, f : f + 512], preferred_element_type=F32)
                h = 0.5 * u
                t = jnp.tanh(u * (0.7978845608028654 + 0.035677408136300125 * (u * u)))
                part = jnp.dot(
                    (h + h * t).astype(BF16), contract[f : f + 512, :], preferred_element_type=F32
                )
                update = part if update is None else update + part
            for b in range(2):
                part = update[b * tile : (b + 1) * tile]
                for k in range(3):
                    state[k, 2 * a + b, at, :] = (
                        state_in[k, 2 * a + b, at, :]
                        + share[2 * a + b, at, :] * part[:, k * 128 : (k + 1) * 128]
                    )
            return 0

        lax.fori_loop(0, USED // tile, mlp, 0)

    if not last:
        for q in range(4):
            for k in range(3):
                state[k, q, USED:NM, :] = jnp.zeros((NM - USED, 128), F32)
        strips(state, share, row_strip, col_strip, corner, tmp)
        return

    def natural(big, _):
        at = pl.ds(pl.multiple_of(big * NR, NR), NR)
        for b in range(2):
            for k in range(3):
                for a in range(2):
                    tmp[pl.ds(a, NR, stride=2), :] = state[k, 2 * a + b, at, :]
                out[2 * big + b, :, k * 128 : (k + 1) * 128] = tmp[0:ROWS, :].astype(BF16)
        return 0

    lax.fori_loop(0, HALF, natural, 0)


def vmem():
    return pl.BlockSpec(memory_space=pltpu.VMEM)


def smem():
    return pl.BlockSpec(memory_space=pltpu.SMEM)


def shape(*dims, dtype=F32):
    return jax.ShapeDtypeStruct(dims, dtype)


STATE = shape(3, 4, NM, 128)
SHARE = shape(4, NM, 128)
STRIPS = [
    shape(2, 3, 2, NT, CH, dtype=BF16),
    shape(2, 3, 2, NR, CH, dtype=BF16),
    shape(2, 2, 16, CH, dtype=BF16),
]


def remap_state(picks, sea_mask, atmos, ocean, flux_weight):
    return pl.pallas_call(
        flux_kernel,
        out_shape=[STATE, SHARE, *STRIPS],
        in_specs=[smem(), smem(), vmem(), vmem(), vmem()],
        out_specs=[vmem()] * 5,
        scratch_shapes=[
            pltpu.VMEM((3, 4 * CELLS + 8, 128), F32),
            pltpu.VMEM((3, 2, CELLS, 128), BF16),
            pltpu.VMEM((3, 2, CELLS, 128), BF16),
            pltpu.VMEM((4, NM, 128), F32),
            pltpu.VMEM((96, 128), F32),
            pltpu.SemaphoreType.DMA((3, 2)),
            pltpu.SemaphoreType.DMA((3, 2)),
        ],
        compiler_params=pltpu.CompilerParams(
            collective_id=0, has_side_effects=True, vmem_limit_bytes=VLIMIT
        ),
    )(picks, sea_mask, atmos, ocean, flux_weight)


def exchange(fold, pieces):
    return pl.pallas_call(
        halo_kernel,
        out_shape=[*STRIPS, shape(3, 2, NT, CH, dtype=BF16)],
        in_specs=[smem(), vmem(), vmem(), vmem()],
        out_specs=[vmem()] * 4,
        scratch_shapes=[
            pltpu.VMEM((LONS, 3, 2, NT, CH), BF16),
            pltpu.SemaphoreType.DMA((8,)),
            pltpu.SemaphoreType.DMA((8,)),
            pltpu.SemaphoreType.DMA((LONS,)),
            pltpu.SemaphoreType.DMA((LONS,)),
        ],
        compiler_params=pltpu.CompilerParams(
            collective_id=1, has_side_effects=True, vmem_limit_bytes=VLIMIT
        ),
    )(fold, *pieces)


def block(index, last, state, share, halos, taps, gain, expand, contract):
    outs = [shape(COLS, ROWS, CH, dtype=BF16)] if last else [STATE, *STRIPS]
    scratch = [pltpu.VMEM(STATE.shape, F32)] if last else []
    return pl.pallas_call(
        functools.partial(block_kernel, index, last),
        out_shape=outs,
        in_specs=[vmem()] * 8 + [pl.BlockSpec(memory_space=pl.ANY)] * 2,
        out_specs=[vmem()] * len(outs),
        scratch_shapes=scratch
        + [
            pltpu.VMEM((4, QR * QT, 128), F32),
            pltpu.VMEM((2, 2, QR * NT, 128), F32),
            pltpu.VMEM((2, NT * NR, 1024), BF16),
            pltpu.VMEM((2, 4, 1024, 256), BF16),
            pltpu.VMEM((6, NM, 256), F32),
            pltpu.VMEM((96, 128), F32),
            pltpu.VMEM((6, 72, 128), F32),
            pltpu.VMEM((CH, FF), BF16),
            pltpu.VMEM((FF, CH), BF16),
            pltpu.SemaphoreType.DMA((2,)),
        ],
        compiler_params=pltpu.CompilerParams(vmem_limit_bytes=VLIMIT),
    )(state, share, *halos, taps, gain, expand, contract)


def body(atmos, ocean, remap, fold, sea_mask, flux_weight, dw_kernel, norm_gain, w_in, w_out):
    band = lax.axis_index(("sec", "lat"))
    lon = lax.axis_index("lon")
    row = remap // NLON
    col = (remap - row * NLON - lon * COLS + HALF + NLON) % NLON
    picks = jnp.where(sea_mask == 0, 4 * CELLS, col * ROWS + row - band * ROWS)
    atmos = atmos.transpose(1, 0, 2).reshape(COLS * ROWS, CA)
    ocean = ocean.transpose(1, 0, 2)
    gain = norm_gain.reshape(2, 1, CH)
    state, share, *pieces = remap_state(picks, sea_mask, atmos, ocean, flux_weight)
    halos = exchange(fold, pieces)
    state, *pieces = block(0, False, state, share, halos, dw_kernel, gain, w_in, w_out)
    halos = exchange(fold, pieces)
    (out,) = block(1, True, state, share, halos, dw_kernel, gain, w_in, w_out)
    return out.transpose(1, 0, 2)


def solution(mesh):
    return jax.shard_map(
        body,
        mesh=mesh,
        in_specs=(
            P(("sec", "lat"), "lon", None),
            P(("sec", "lat"), "lon", None),
            P(("sec", "lat"), "lon"),
            P("lon"),
            P(("sec", "lat"), "lon"),
            P(),
            P(),
            P(),
            P(),
            P(),
        ),
        out_specs=P(("sec", "lat"), "lon", None),
        check_vma=False,
    )
```

```python
import functools

import jax
import jax.numpy as jnp
from jax import lax
from jax.experimental import pallas as pl
from jax.experimental.pallas import tpu as pltpu
from jax.sharding import PartitionSpec as P

ROWS, COLS, CH, CA, FF = 32, 90, 384, 512, 1536
HALF = 45
CELLS = ROWS * HALF
BANDS, LONS = 8, 16
NLON = COLS * LONS
NR, NT, NM, USED = 16, 48, 768, 720
QR, QT = 24, 50
LOW = ((0, 0), (1, 0), (0, 1))
ROW_HIGH = ((1, 14), (0, 15), (1, 15))
COL_HIGH = ((1, 43), (0, 44), (1, 44))
ROW_TOP = ((1, 17), (0, 18), (1, 18))
COL_TOP = ((1, 46), (0, 47), (1, 47))
MESH = pl.DeviceIdType.MESH
F32, BF16 = jnp.float32, jnp.bfloat16
VLIMIT = 60 * 2**20


def lane_low(shape):
    return lax.broadcasted_iota(jnp.int32, shape, len(shape) - 1) < 64


def strips(state, share, row_strip, col_strip, corner, tmp):
    for k in range(3):
        lanes = slice(k * 128, (k + 1) * 128)
        for side, edge in enumerate((LOW, ROW_HIGH)):
            for n, (a, big) in enumerate(edge):
                for b in range(2):
                    at = pl.ds(big, NT, stride=NR)
                    row_strip[side, n, b, :, lanes] = (
                        state[k, 2 * a + b, at, :] * share[2 * a + b, at, :]
                    ).astype(BF16)
        for side, edge in enumerate((LOW, COL_HIGH)):
            for n, (b, big) in enumerate(edge):
                for a in range(2):
                    at = slice(big * NR, (big + 1) * NR)
                    col_strip[side, n, a, :, lanes] = (
                        state[k, 2 * a + b, at, :] * share[2 * a + b, at, :]
                    ).astype(BF16)
        for rside, redge in enumerate((LOW, ROW_HIGH)):
            for cside, cedge in enumerate((LOW, COL_HIGH)):
                for n, (a, rbig) in enumerate(redge):
                    for m, (b, cbig) in enumerate(cedge):
                        at = slice(cbig * NR + rbig, cbig * NR + rbig + 1)
                        tmp[3 * n + m : 3 * n + m + 1, :] = (
                            state[k, 2 * a + b, at, :] * share[2 * a + b, at, :]
                        )
                corner[rside, cside, :, lanes] = tmp[0:16, :].astype(BF16)


def flux_kernel(
    picks, sea, atmos, ocean, weight,
    state, share, row_strip, col_strip, corner,
    table, outgoing, incoming, taken, tmp, send_sem, recv_sem,
):
    sec, lat, lon = (lax.axis_index(n) for n in ("sec", "lat", "lon"))
    left, right = lax.rem(lon + LONS - 1, LONS), lax.rem(lon + 1, LONS)
    barrier = pltpu.get_barrier_semaphore()
    for other in (left, right):
        pl.semaphore_signal(barrier, inc=1, device_id=(sec, lat, other), device_id_type=MESH)
    pl.semaphore_wait(barrier, 2)

    def copy(k, side):
        return pltpu.make_async_remote_copy(
            src_ref=outgoing.at[k, side],
            dst_ref=incoming.at[k, 1 - side],
            send_sem=send_sem.at[k, side],
            recv_sem=recv_sem.at[k, 1 - side],
            device_id=(sec, lat, (left, right)[side]),
            device_id_type=MESH,
        )

    for k in range(3):
        for side in range(2):

            def cells(i, _, k=k, side=side):
                at = pl.multiple_of(i * 288, 288)
                value = jnp.dot(
                    atmos[pl.ds(side * CELLS + at, 288), :],
                    weight[:, k * 128 : (k + 1) * 128],
                    preferred_element_type=F32,
                ).astype(BF16)
                outgoing[k, side, pl.ds(at, 288), :] = value
                table[k, pl.ds((1 + side) * CELLS + at, 288), :] = value.astype(F32)
                return 0

            lax.fori_loop(0, CELLS // 288, cells, 0)
            copy(k, side).start()
        table[k, 4 * CELLS : 4 * CELLS + 8, :] = jnp.zeros((8, 128), F32)

    tail = slice(USED, NM)
    for q in range(4):
        share[q, tail, :] = jnp.zeros((NM - USED, 128), F32)
        for k in range(3):
            state[k, q, tail, :] = jnp.zeros((NM - USED, 128), F32)
    tmp[...] = jnp.zeros_like(tmp)

    def ocean_cells(big, _):
        at = pl.ds(pl.multiple_of(big * NR, NR), NR)
        for b in range(2):
            for k in range(3):
                tmp[0:ROWS, :] = ocean[2 * big + b, :, k * 128 : (k + 1) * 128].astype(F32)
                for a in range(2):
                    state[k, 2 * a + b, at, :] = tmp[pl.ds(a, NR, stride=2), :]
        return 0

    lax.fori_loop(0, HALF, ocean_cells, 0)
    tmp[0:1, :] = jnp.zeros((1, 128), F32)
    tmp[1:2, :] = jnp.ones((1, 128), F32)

    def share_cells(big, _):
        base = pl.multiple_of(big * NR, NR)
        for a in range(2):
            for b in range(2):
                for r in range(NR):
                    share[2 * a + b, pl.ds(base + r, 1), :] = tmp[
                        pl.ds(sea[2 * r + a, 2 * big + b], 1), :
                    ]
        return 0

    lax.fori_loop(0, HALF, share_cells, 0)

    for k in range(3):
        for side in range(2):
            copy(k, 1 - side).wait_recv()

            def widened(i, _, k=k, side=side):
                at = pl.multiple_of(i * 288, 288)
                table[k, pl.ds(3 * side * CELLS + at, 288), :] = incoming[
                    k, side, pl.ds(at, 288), :
                ].astype(F32)
                return 0

            lax.fori_loop(0, CELLS // 288, widened, 0)

        def gather_cells(big, _, k=k):
            base = pl.multiple_of(big * NR, NR)
            for a in range(2):
                for b in range(2):
                    for r in range(NR):
                        taken[2 * a + b, pl.ds(base + r, 1), :] = table[
                            k, pl.ds(picks[2 * r + a, 2 * big + b], 1), :
                        ]
            return 0

        lax.fori_loop(0, HALF, gather_cells, 0)
        for q in range(4):
            state[k, q, 0:USED, :] += taken[q, 0:USED, :]
    strips(state, share, row_strip, col_strip, corner, tmp)
    for k in range(3):
        for side in range(2):
            copy(k, side).wait_send()


def block_kernel(
    index, last, fold, row_out, col_out, corner_out, state_in, share, kernel_taps, gain, expand_all, contract_all, *rest
):
    (
        *rest, row_halo, col_halo, corner_halo, ring, padded, paired, lhs, rhs, conv, tmp, taps, folded, expand, contract,
        load_sem, send_sem, recv_sem, ring_send, ring_recv,
    ) = rest
    if last:
        out, state = rest
    else:
        state, row_strip, col_strip, corner = rest
    loads = [
        pltpu.make_async_copy(expand_all.at[index], expand, load_sem.at[0]),
        pltpu.make_async_copy(contract_all.at[index], contract, load_sem.at[1]),
    ]
    for load in loads:
        load.start()

    sec, lat, lon = (lax.axis_index(n) for n in ("sec", "lat", "lon"))
    band = sec * 4 + lat
    chip, core = lon // 2, lax.rem(lon, 2)
    sibling = lon + 1 - 2 * core
    left, right = lax.rem(lon + LONS - 1, LONS), lax.rem(lon + 1, LONS)
    has_north, has_south, top = band < BANDS - 1, band > 0, band == BANDS - 1

    def place(step, where):
        other = band + step
        return (other // 4, lax.rem(other, 4), where)

    def peer(step):
        return (sec, lat, lax.rem(lon + 2 * step, LONS))

    barrier = pltpu.get_barrier_semaphore()

    def greet(device):
        pl.semaphore_signal(barrier, inc=1, device_id=device, device_id_type=MESH)

    greet((sec, lat, left))
    greet((sec, lat, right))
    pl.when(has_north)(lambda: [greet(place(1, w)) for w in (left, lon, right)] and None)
    pl.when(has_south)(lambda: [greet(place(-1, w)) for w in (left, lon, right)] and None)
    pl.when(top)(lambda: [greet(peer(s)) for s in range(1, 8)] and None)
    greeted = 2 + jnp.where(has_north, 3, 0) + jnp.where(has_south, 3, 0) + jnp.where(top, 7, 0)
    pl.semaphore_wait(barrier, greeted)

    def copy(n, src, dst, device):
        return pltpu.make_async_remote_copy(
            src_ref=src, dst_ref=dst, send_sem=send_sem.at[n], recv_sem=recv_sem.at[n],
            device_id=device, device_id_type=MESH,
        )

    def sideways():
        return [
            copy(0, col_out.at[1], col_halo.at[0], (sec, lat, right)),
            copy(1, col_out.at[0], col_halo.at[1], (sec, lat, left)),
        ]

    def up():
        return [
            copy(2, row_out.at[1], row_halo.at[0], place(1, lon)),
            copy(3, corner_out.at[1, 0], corner_halo.at[0, 1], place(1, left)),
            copy(4, corner_out.at[1, 1], corner_halo.at[0, 0], place(1, right)),
        ]

    def down():
        return [
            copy(5, row_out.at[0], row_halo.at[1], place(-1, lon)),
            copy(6, corner_out.at[0, 0], corner_halo.at[1, 1], place(-1, left)),
            copy(7, corner_out.at[0, 1], corner_halo.at[1, 0], place(-1, right)),
        ]

    def ring_copy(step):
        return pltpu.make_async_remote_copy(
            src_ref=row_out.at[1], dst_ref=ring.at[core, chip],
            send_sem=ring_send.at[step], recv_sem=ring_recv.at[step],
            device_id=peer(step), device_id_type=MESH,
        )

    def forward():
        return pltpu.make_async_remote_copy(
            src_ref=ring.at[core], dst_ref=ring.at[core],
            send_sem=ring_send.at[0], recv_sem=ring_recv.at[0],
            device_id=(sec, lat, sibling), device_id_type=MESH,
        )

    def start(copies):
        for c in copies:
            c.start()

    start(sideways())
    pl.when(has_north)(lambda: start(up()))
    pl.when(has_south)(lambda: start(down()))
    pl.when(top)(lambda: start([ring_copy(s) for s in (4, 3, 5, 2, 6, 1, 7)]))

    @pl.when(jnp.logical_not(has_south))
    def _():
        row_halo[0] = jnp.zeros(row_halo.shape[1:], BF16)
        corner_halo[0] = jnp.zeros(corner_halo.shape[1:], BF16)

    @pl.when(top)
    def _():
        row_halo[1] = jnp.zeros(row_halo.shape[1:], BF16)
        corner_halo[1] = jnp.zeros(corner_halo.shape[1:], BF16)
        ring[core, chip] = row_out[1]

    padded[...] = jnp.zeros_like(padded)
    conv[:, :, USED:NM, :] = jnp.zeros((6, 2, NM - USED, 128), F32)
    taps[...] = jnp.zeros_like(taps)
    tmp[0:16, :] = jnp.zeros((16, 128), F32)
    low8 = lane_low((8, 128))
    for row in range(7):
        for k in range(3):
            tmp[1:8, :] = kernel_taps[index, row, :, k * 128 : (k + 1) * 128]
            now, before = tmp[1:9, :], tmp[0:8, :]
            at = slice(8 * (row + 1), 8 * (row + 2))
            taps[2 * k, at, :] = jnp.where(low8, now, pltpu.roll(before, 64, 1))
            taps[2 * k + 1, at, :] = jnp.where(low8, pltpu.roll(now, 64, 1), before)

    def weights(i, _):
        dr, dt = i // 4, lax.rem(i, 4)
        diag = (
            lax.broadcasted_iota(jnp.int32, (64, 128), 0)
            == lax.broadcasted_iota(jnp.int32, (64, 128), 1) % 64
        )
        for g in range(6):
            for pa in range(2):
                for pb in range(2):
                    to = pl.ds(pl.multiple_of(dr * 256 + pa * 128 + pb * 64, 64), 64)
                    for r in range(2):
                        at = (2 * dr + pa + 1 - r) * 8 + 2 * dt + pb
                        value = jnp.where(diag, taps[g, pl.ds(at, 1), :], 0.0)
                        rhs[g, dt, to, r * 128 : (r + 1) * 128] = value.astype(BF16)
        return 0

    lax.fori_loop(0, 16, weights, 0)

    def arrived(copies):
        for c in copies:
            c.wait_recv()

    arrived(sideways())
    pl.when(has_north)(lambda: arrived(down()))
    pl.when(has_south)(lambda: arrived(up()))

    for k in range(3):
        lanes = slice(k * 128, (k + 1) * 128)

        def own(big, _, k=k):
            src = pl.ds(pl.multiple_of(big * NR, NR), NR)
            for a in range(2):
                for b in range(2):
                    value = state_in[k, 2 * a + b, src, :] * share[2 * a + b, src, :]
                    padded[2 * (1 - a) + 1 - b, pl.ds((big + 1 + b) * QR + 1 + a, NR), :] = value
            return 0

        lax.fori_loop(0, HALF, own, 0)
        for side, places in enumerate((LOW, ROW_TOP)):
            for n, (pa, pr) in enumerate(places):
                for b in range(2):
                    padded[2 * pa + 1 - b, pl.ds((1 + b) * QR + pr, NT, stride=QR), :] = row_halo[
                        side, n, b, :, lanes
                    ].astype(F32)
        for side, places in enumerate((LOW, COL_TOP)):
            for n, (pb, pt) in enumerate(places):
                for a in range(2):
                    at = pt * QR + 1 + a
                    padded[2 * (1 - a) + pb, at : at + NR, :] = col_halo[
                        side, n, a, :, lanes
                    ].astype(F32)
        for rside, rplaces in enumerate((LOW, ROW_TOP)):
            for cside, cplaces in enumerate((LOW, COL_TOP)):
                tmp[0:16, :] = corner_halo[rside, cside, :, lanes].astype(F32)
                for n, (pa, pr) in enumerate(rplaces):
                    for m, (pb, pt) in enumerate(cplaces):
                        at = pt * QR + pr
                        padded[2 * pa + pb, at : at + 1, :] = tmp[3 * n + m : 3 * n + m + 1, :]

        def pair_up(big, _):
            at = pl.ds(pl.multiple_of(big * 8 * QR, 8 * QR), 8 * QR)
            low = lane_low((8 * QR, 128))
            for pa in range(2):
                even, odd = padded[2 * pa, at, :], padded[2 * pa + 1, at, :]
                paired[0, pa, at, :] = jnp.where(low, even, pltpu.roll(odd, 64, 1))
                paired[1, pa, at, :] = jnp.where(low, pltpu.roll(even, 64, 1), odd)
            return 0

        lax.fori_loop(0, NT // 8, pair_up, 0)

        def spread(big, _):
            to = pl.ds(pl.multiple_of(big * NR, NR), NR)
            for g in range(2):
                for d in range(4):
                    for pa in range(2):
                        c0 = d * 256 + pa * 128
                        lhs[g, to, c0 : c0 + 128] = paired[
                            g, pa, pl.ds(big * QR + d, NR), :
                        ].astype(BF16)
            return 0

        lax.fori_loop(0, NT, spread, 0)
        for g in range(2):
            total = None
            for d in range(4):
                part = jnp.dot(
                    lhs[g, d * NR : d * NR + USED, :], rhs[2 * k + g, d], preferred_element_type=F32
                )
                total = part if total is None else total + part
            for a in range(2):
                conv[2 * k + g, a, 0:USED, :] = total[:, a * 128 : (a + 1) * 128]

    @pl.when(top)
    def _():
        for s in range(1, 8):
            ring_copy(s).wait_recv()
        forward().start()

    for load in loads:
        load.wait()

    def conv_rows(a, at, count):
        low = lane_low((count, 128))
        chunks = []
        for k in range(3):
            even, odd = conv[2 * k, a, at, :], conv[2 * k + 1, a, at, :]
            chunks.append(
                [
                    jnp.where(low, even, pltpu.roll(odd, 64, 1)),
                    jnp.where(low, pltpu.roll(even, 64, 1), odd),
                ]
            )
        return chunks

    def feed(chunks):
        centre = jnp.sum(chunks[0] + chunks[1] + chunks[2], axis=1, keepdims=True) * (1.0 / CH)
        chunks = [c - centre for c in chunks]
        squares = chunks[0] * chunks[0] + chunks[1] * chunks[1] + chunks[2] * chunks[2]
        scale = lax.rsqrt(jnp.sum(squares, axis=1, keepdims=True) * (1.0 / CH) + 1e-06)
        normed = jnp.concatenate(
            [
                (c * scale * gain[index, :, k * 128 : (k + 1) * 128]).astype(BF16)
                for k, c in enumerate(chunks)
            ],
            axis=1,
        )
        update = None
        for f in range(0, FF, 512):
            u = jnp.dot(normed, expand[:, f : f + 512], preferred_element_type=F32)
            h = 0.5 * u
            t = jnp.tanh(u * (0.7978845608028654 + 0.035677408136300125 * (u * u)))
            part = jnp.dot(
                (h + h * t).astype(BF16), contract[f : f + 512, :], preferred_element_type=F32
            )
            update = part if update is None else update + part
        return update

    def advance(a, b, at, update):
        for k in range(3):
            state[k, 2 * a + b, at, :] = (
                state_in[k, 2 * a + b, at, :]
                + share[2 * a + b, at, :] * update[:, k * 128 : (k + 1) * 128]
            )

    tile = 240
    for a in range(2):
        for i in range(USED // tile):
            at = slice(i * tile, (i + 1) * tile)
            update = feed([jnp.concatenate(c, axis=0) for c in conv_rows(a, at, tile)])
            for b in range(2):
                advance(a, b, at, update[b * tile : (b + 1) * tile])
    for q in range(4):
        for k in range(3):
            state[k, q, USED:NM, :] = jnp.zeros((NM - USED, 128), F32)

    @pl.when(top)
    def _():
        forward().wait()
        first = lax.rem(fold[0] - 92 + NLON, NLON)
        sector = lax.div(first, COLS)
        off = first - sector * COLS
        at_out = lax.broadcasted_iota(jnp.int32, (2 * NT, 2 * NT), 0)
        at_in = lax.broadcasted_iota(jnp.int32, (2 * NT, 2 * NT), 1)
        wanted = off + 95 - jnp.where(at_out >= NT, 2 * (at_out - NT) + 1, 2 * at_out)
        pair = jnp.where(at_in >= NT, at_in - NT, at_in)
        column = 2 * pair + jnp.where(at_in >= NT, 1, 0)
        low = lane_low((56, 128))
        folded[...] = jnp.zeros_like(folded)
        for n in range(3):
            got = jnp.zeros((2 * NT, CH), F32)
            for s in range(3):
                from_sector = lax.rem(sector + s, LONS)
                pick = jnp.where((column + s * COLS == wanted) & (pair < HALF), 1.0, 0.0).astype(BF16)
                strip = ring[lax.rem(from_sector, 2), lax.div(from_sector, 2), 2 - n]
                got += jnp.dot(pick, strip.reshape(2 * NT, CH), preferred_element_type=F32)
            for k in range(3):
                for pb in range(2):
                    tmp[0:NT, :] = got[pb * NT : (pb + 1) * NT, k * 128 : (k + 1) * 128]
                    tmp[NT:56, :] = jnp.zeros((8, 128), F32)
                    value = tmp[0:56, :]
                    turned = pltpu.roll(value, 64, 1)
                    folded[2 * k, n, pb] = jnp.where(low, value, turned)
                    folded[2 * k + 1, n, pb] = jnp.where(low, turned, value)

        def correct(g, _):
            for i, (a, big) in enumerate(ROW_HIGH):
                at = pl.ds(big, NT, stride=NR)
                total = conv[g, a, at, :]
                for n in range(i + 1):
                    tap_row = 6 + n - i
                    for e in range(8):
                        total += (
                            folded[g, n, e % 2, e // 2 : e // 2 + NT, :]
                            * taps[g, 8 * (tap_row + 1) + e : 8 * (tap_row + 1) + e + 1, :]
                        )
                conv[g, a, at, :] = total
            return 0

        lax.fori_loop(0, 6, correct, 0)
        picked = [conv_rows(a, pl.ds(big, NT, stride=NR), NT) for a, big in ROW_HIGH]
        update = feed([jnp.concatenate([p[k][b] for p in picked for b in range(2)], axis=0) for k in range(3)])
        for i, (a, big) in enumerate(ROW_HIGH):
            for b in range(2):
                at = (2 * i + b) * NT
                advance(a, b, pl.ds(big, NT, stride=NR), update[at : at + NT])

    def sent(copies):
        for c in copies:
            c.wait_send()

    sent(sideways())
    pl.when(has_north)(lambda: sent(up()))
    pl.when(has_south)(lambda: sent(down()))
    pl.when(top)(lambda: sent([ring_copy(s) for s in range(1, 8)]))

    if not last:
        strips(state, share, row_strip, col_strip, corner, tmp)
        return

    def natural(big, _):
        at = pl.ds(pl.multiple_of(big * NR, NR), NR)
        for b in range(2):
            for k in range(3):
                for a in range(2):
                    tmp[pl.ds(a, NR, stride=2), :] = state[k, 2 * a + b, at, :]
                out[2 * big + b, :, k * 128 : (k + 1) * 128] = tmp[0:ROWS, :].astype(BF16)
        return 0

    lax.fori_loop(0, HALF, natural, 0)


def vmem():
    return pl.BlockSpec(memory_space=pltpu.VMEM)


def smem():
    return pl.BlockSpec(memory_space=pltpu.SMEM)


def shape(*dims, dtype=F32):
    return jax.ShapeDtypeStruct(dims, dtype)


STATE = shape(3, 4, NM, 128)
SHARE = shape(4, NM, 128)
STRIPS = [
    shape(2, 3, 2, NT, CH, dtype=BF16),
    shape(2, 3, 2, NR, CH, dtype=BF16),
    shape(2, 2, 16, CH, dtype=BF16),
]


def remap_state(picks, sea_mask, atmos, ocean, flux_weight):
    return pl.pallas_call(
        flux_kernel,
        out_shape=[STATE, SHARE, *STRIPS],
        in_specs=[smem(), smem(), vmem(), vmem(), vmem()],
        out_specs=[vmem()] * 5,
        scratch_shapes=[
            pltpu.VMEM((3, 4 * CELLS + 8, 128), F32),
            pltpu.VMEM((3, 2, CELLS, 128), BF16),
            pltpu.VMEM((3, 2, CELLS, 128), BF16),
            pltpu.VMEM((4, NM, 128), F32),
            pltpu.VMEM((96, 128), F32),
            pltpu.SemaphoreType.DMA((3, 2)),
            pltpu.SemaphoreType.DMA((3, 2)),
        ],
        compiler_params=pltpu.CompilerParams(
            collective_id=0, has_side_effects=True, vmem_limit_bytes=VLIMIT
        ),
    )(picks, sea_mask, atmos, ocean, flux_weight)


def block(index, last, fold, pieces, state, share, taps, gain, expand, contract):
    outs = [shape(COLS, ROWS, CH, dtype=BF16)] if last else [STATE, *STRIPS]
    scratch = [pltpu.VMEM(STATE.shape, F32)] if last else []
    return pl.pallas_call(
        functools.partial(block_kernel, index, last),
        out_shape=outs,
        in_specs=[smem()] + [vmem()] * 7 + [pl.BlockSpec(memory_space=pl.ANY)] * 2,
        out_specs=[vmem()] * len(outs),
        scratch_shapes=scratch
        + [pltpu.VMEM(s.shape, BF16) for s in STRIPS]
        + [
            pltpu.VMEM((2, LONS // 2, 3, 2, NT, CH), BF16),
            pltpu.VMEM((4, QR * QT, 128), F32),
            pltpu.VMEM((2, 2, QR * NT, 128), F32),
            pltpu.VMEM((2, NT * NR, 1024), BF16),
            pltpu.VMEM((6, 4, 1024, 256), BF16),
            pltpu.VMEM((6, 2, NM, 128), F32),
            pltpu.VMEM((96, 128), F32),
            pltpu.VMEM((6, 72, 128), F32),
            pltpu.VMEM((6, 3, 2, 56, 128), F32),
            pltpu.VMEM((CH, FF), BF16),
            pltpu.VMEM((FF, CH), BF16),
            pltpu.SemaphoreType.DMA((2,)),
            pltpu.SemaphoreType.DMA((8,)),
            pltpu.SemaphoreType.DMA((8,)),
            pltpu.SemaphoreType.DMA((8,)),
            pltpu.SemaphoreType.DMA((8,)),
        ],
        compiler_params=pltpu.CompilerParams(
            collective_id=1 + index, has_side_effects=True, vmem_limit_bytes=VLIMIT
        ),
    )(fold, *pieces, state, share, taps, gain, expand, contract)


def body(atmos, ocean, remap, fold, sea_mask, flux_weight, dw_kernel, norm_gain, w_in, w_out):
    band = lax.axis_index(("sec", "lat"))
    lon = lax.axis_index("lon")
    row = remap // NLON
    col = (remap - row * NLON - lon * COLS + HALF + NLON) % NLON
    picks = jnp.where(sea_mask == 0, 4 * CELLS, col * ROWS + row - band * ROWS)
    atmos = atmos.transpose(1, 0, 2).reshape(COLS * ROWS, CA)
    ocean = ocean.transpose(1, 0, 2)
    gain = norm_gain.reshape(2, 1, CH)
    state, share, *pieces = remap_state(picks, sea_mask, atmos, ocean, flux_weight)
    state, *pieces = block(0, False, fold, pieces, state, share, dw_kernel, gain, w_in, w_out)
    (out,) = block(1, True, fold, pieces, state, share, dw_kernel, gain, w_in, w_out)
    return out.transpose(1, 0, 2)


def solution(mesh):
    return jax.shard_map(
        body,
        mesh=mesh,
        in_specs=(
            P(("sec", "lat"), "lon", None),
            P(("sec", "lat"), "lon", None),
            P(("sec", "lat"), "lon"),
            P("lon"),
            P(("sec", "lat"), "lon"),
            P(),
            P(),
            P(),
            P(),
            P(),
        ),
        out_specs=P(("sec", "lat"), "lon", None),
        check_vma=False,
    )
```

```python
import jax
import jax.numpy as jnp
from jax import lax
from jax.experimental import pallas as pl
from jax.experimental.pallas import tpu as pltpu
from jax.sharding import PartitionSpec as P

ROWS, COLS, CH, CA, FF = 32, 90, 384, 512, 1536
HALF = 45
CELLS = ROWS * HALF
BANDS, LONS = 8, 16
NLON = COLS * LONS
NR, NT, NM, USED = 16, 48, 768, 720
QR, QT = 24, 50
LOW = ((0, 0), (1, 0), (0, 1))
ROW_HIGH = ((1, 14), (0, 15), (1, 15))
COL_HIGH = ((1, 43), (0, 44), (1, 44))
ROW_TOP = ((1, 17), (0, 18), (1, 18))
COL_TOP = ((1, 46), (0, 47), (1, 47))
MESH = pl.DeviceIdType.MESH
F32, BF16 = jnp.float32, jnp.bfloat16
VLIMIT = 60 * 2**20


def lane_low(shape):
    return lax.broadcasted_iota(jnp.int32, shape, len(shape) - 1) < 64


def ocean_kernel(
    picks, sea, fold, weight, kernel_taps, gain, atmos_in, ocean_in, expand_all, contract_all,
    out,
    atmos, ocean, table, outgoing, incoming, state, share, row_out, col_out, corner_out, row_halo, col_halo, corner_halo,
    ring_first, ring_second, padded, paired, lhs, rhs, tmp, taps, folded, saved, expand, contract,
    load_sem, flux_send, flux_recv, halo_send, halo_recv, ring_send, ring_recv,
):
    ring = (ring_first, ring_second)

    def load(n, src, dst):
        return pltpu.make_async_copy(src, dst, load_sem.at[n])

    atmos_loads = [
        load(side, atmos_in.at[pl.ds(side * CELLS, CELLS)], atmos.at[pl.ds(side * CELLS, CELLS)])
        for side in range(2)
    ]
    ocean_load = load(2, ocean_in, ocean)

    def mlp_loads(blk):
        return [load(3, expand_all.at[blk], expand), load(4, contract_all.at[blk], contract)]

    def start(copies):
        for c in copies:
            c.start()

    def arrived(copies):
        for c in copies:
            c.wait_recv()

    def sent(copies):
        for c in copies:
            c.wait_send()

    start(atmos_loads)
    ocean_load.start()
    start(mlp_loads(0))

    sec, lat, lon = (lax.axis_index(n) for n in ("sec", "lat", "lon"))
    band = sec * 4 + lat
    chip, core = lon // 2, lax.rem(lon, 2)
    sibling = lon + 1 - 2 * core
    left, right = lax.rem(lon + LONS - 1, LONS), lax.rem(lon + 1, LONS)
    has_north, has_south, top = band < BANDS - 1, band > 0, band == BANDS - 1

    def place(step, where):
        other = band + step
        return (other // 4, lax.rem(other, 4), where)

    def peer(step):
        return (sec, lat, lax.rem(lon + 2 * step, LONS))

    barrier = pltpu.get_barrier_semaphore()

    def greet(device):
        pl.semaphore_signal(barrier, inc=1, device_id=device, device_id_type=MESH)

    greet((sec, lat, left))
    greet((sec, lat, right))
    pl.when(has_north)(lambda: [greet(place(1, w)) for w in (left, lon, right)] and None)
    pl.when(has_south)(lambda: [greet(place(-1, w)) for w in (left, lon, right)] and None)
    pl.when(top)(lambda: [greet(peer(s)) for s in range(1, 8)] and None)
    greeted = 2 + jnp.where(has_north, 3, 0) + jnp.where(has_south, 3, 0) + jnp.where(top, 7, 0)
    pl.semaphore_wait(barrier, greeted)

    def flux_copy(k, side):
        return pltpu.make_async_remote_copy(
            src_ref=outgoing.at[k, side], dst_ref=incoming.at[k, 1 - side],
            send_sem=flux_send.at[k, side], recv_sem=flux_recv.at[k, 1 - side],
            device_id=(sec, lat, (left, right)[side]), device_id_type=MESH,
        )

    for k in range(3):
        for side in range(2):
            if k == 0:
                atmos_loads[side].wait()

            def cells(i, _, k=k, side=side):
                at = pl.multiple_of(i * 288, 288)
                value = jnp.dot(
                    atmos[pl.ds(side * CELLS + at, 288), :],
                    weight[:, k * 128 : (k + 1) * 128],
                    preferred_element_type=F32,
                ).astype(BF16)
                outgoing[k, side, pl.ds(at, 288), :] = value
                table[k, pl.ds((1 + side) * CELLS + at, 288), :] = value.astype(F32)
                return 0

            lax.fori_loop(0, CELLS // 288, cells, 0)
            flux_copy(k, side).start()
        table[k, 4 * CELLS : 4 * CELLS + 8, :] = jnp.zeros((8, 128), F32)

    for q in range(4):
        share[q, USED:NM, :] = jnp.zeros((NM - USED, 128), F32)
        for k in range(3):
            state[k, q, USED:NM, :] = jnp.zeros((NM - USED, 128), F32)
    tmp[...] = jnp.zeros_like(tmp)
    tmp[1:2, :] = jnp.ones((1, 128), F32)

    def share_cells(big, _):
        base = pl.multiple_of(big * NR, NR)
        for a in range(2):
            for b in range(2):
                for r in range(NR):
                    share[2 * a + b, pl.ds(base + r, 1), :] = tmp[
                        pl.ds(sea[2 * r + a, 2 * big + b], 1), :
                    ]
        return 0

    lax.fori_loop(0, HALF, share_cells, 0)
    ocean_load.wait()

    def ocean_cells(big, _):
        at = pl.ds(pl.multiple_of(big * NR, NR), NR)
        for b in range(2):
            for k in range(3):
                tmp[0:ROWS, :] = ocean[2 * big + b, :, k * 128 : (k + 1) * 128].astype(F32)
                for a in range(2):
                    state[k, 2 * a + b, at, :] = tmp[pl.ds(a, NR, stride=2), :]
        return 0

    lax.fori_loop(0, HALF, ocean_cells, 0)
    padded[...] = jnp.zeros_like(padded)

    @pl.when(jnp.logical_not(has_south))
    def _():
        for blk in range(2):
            row_halo[blk, :, 0] = jnp.zeros((3, *row_halo.shape[3:]), BF16)
            corner_halo[blk, :, 0] = jnp.zeros((3, *corner_halo.shape[3:]), BF16)

    @pl.when(top)
    def _():
        for blk in range(2):
            row_halo[blk, :, 1] = jnp.zeros((3, *row_halo.shape[3:]), BF16)
            corner_halo[blk, :, 1] = jnp.zeros((3, *corner_halo.shape[3:]), BF16)

    def copy(blk, k, n, src, dst, device):
        return pltpu.make_async_remote_copy(
            src_ref=src, dst_ref=dst, send_sem=halo_send.at[blk, k, n], recv_sem=halo_recv.at[blk, k, n],
            device_id=device, device_id_type=MESH,
        )

    def sideways(blk, k):
        return [
            copy(blk, k, 0, col_out.at[k, 1], col_halo.at[blk, k, 0], (sec, lat, right)),
            copy(blk, k, 1, col_out.at[k, 0], col_halo.at[blk, k, 1], (sec, lat, left)),
        ]

    def up(blk, k):
        return [
            copy(blk, k, 2, row_out.at[k, 1], row_halo.at[blk, k, 0], place(1, lon)),
            copy(blk, k, 3, corner_out.at[k, 1, 0], corner_halo.at[blk, k, 0, 1], place(1, left)),
            copy(blk, k, 4, corner_out.at[k, 1, 1], corner_halo.at[blk, k, 0, 0], place(1, right)),
        ]

    def down(blk, k):
        return [
            copy(blk, k, 5, row_out.at[k, 0], row_halo.at[blk, k, 1], place(-1, lon)),
            copy(blk, k, 6, corner_out.at[k, 0, 0], corner_halo.at[blk, k, 1, 1], place(-1, left)),
            copy(blk, k, 7, corner_out.at[k, 0, 1], corner_halo.at[blk, k, 1, 0], place(-1, right)),
        ]

    def ring_copy(blk, k, step):
        return pltpu.make_async_remote_copy(
            src_ref=row_out.at[k, 1], dst_ref=ring[blk].at[k, core, chip],
            send_sem=ring_send.at[blk, k, step], recv_sem=ring_recv.at[blk, k, step],
            device_id=peer(step), device_id_type=MESH,
        )

    def forward(blk, k):
        return pltpu.make_async_remote_copy(
            src_ref=ring[blk].at[k, core], dst_ref=ring[blk].at[k, core],
            send_sem=ring_send.at[blk, k, 0], recv_sem=ring_recv.at[blk, k, 0],
            device_id=(sec, lat, sibling), device_id_type=MESH,
        )

    def send_edges(blk, k):
        for side, edge in enumerate((LOW, COL_HIGH)):
            for n, (b, big) in enumerate(edge):
                for a in range(2):
                    at = slice(big * NR, (big + 1) * NR)
                    col_out[k, side, n, a] = (
                        state[k, 2 * a + b, at, :] * share[2 * a + b, at, :]
                    ).astype(BF16)
        for side, edge in enumerate((LOW, ROW_HIGH)):
            for n, (a, big) in enumerate(edge):
                for b in range(2):
                    at = pl.ds(big, NT, stride=NR)
                    row_out[k, side, n, b] = (
                        state[k, 2 * a + b, at, :] * share[2 * a + b, at, :]
                    ).astype(BF16)
        tmp[9:16, :] = jnp.zeros((7, 128), F32)
        for rside, redge in enumerate((LOW, ROW_HIGH)):
            for cside, cedge in enumerate((LOW, COL_HIGH)):
                for n, (a, rbig) in enumerate(redge):
                    for m, (b, cbig) in enumerate(cedge):
                        at = slice(cbig * NR + rbig, cbig * NR + rbig + 1)
                        tmp[3 * n + m : 3 * n + m + 1, :] = (
                            state[k, 2 * a + b, at, :] * share[2 * a + b, at, :]
                        )
                corner_out[k, rside, cside] = tmp[0:16, :].astype(BF16)
        start(sideways(blk, k))
        pl.when(has_north)(lambda: start(up(blk, k)))
        pl.when(has_south)(lambda: start(down(blk, k)))

        @pl.when(top)
        def _():
            start([ring_copy(blk, k, s) for s in (4, 3, 5, 2, 6, 1, 7)])
            ring[blk][k, core, chip] = row_out[k, 1]

    def edges_sent(blk, k):
        sent(sideways(blk, k))
        pl.when(has_north)(lambda: sent(up(blk, k)))
        pl.when(has_south)(lambda: sent(down(blk, k)))
        pl.when(top)(lambda: sent([ring_copy(blk, k, s) for s in range(1, 8)]))

    def build_taps(blk):
        taps[...] = jnp.zeros_like(taps)
        tmp[0:16, :] = jnp.zeros((16, 128), F32)
        low = lane_low((8, 128))
        for row in range(7):
            for k in range(3):
                for e in range(7):
                    tmp[1 + e : 2 + e, :] = kernel_taps[row, e, blk : blk + 1, k * 128 : (k + 1) * 128]
                now, before = tmp[1:9, :], tmp[0:8, :]
                at = slice(8 * (row + 1), 8 * (row + 2))
                taps[2 * k, at, :] = jnp.where(low, now, pltpu.roll(before, 64, 1))
                taps[2 * k + 1, at, :] = jnp.where(low, pltpu.roll(now, 64, 1), before)

    def build_weights(blk, k):
        slot = (3 * blk + k) % 2

        def weights(i, _):
            dr, dt = i // 4, lax.rem(i, 4)
            diag = (
                lax.broadcasted_iota(jnp.int32, (64, 128), 0)
                == lax.broadcasted_iota(jnp.int32, (64, 128), 1) % 64
            )
            for g in range(2):
                for pa in range(2):
                    for pb in range(2):
                        to = pl.ds(pl.multiple_of(dr * 256 + pa * 128 + pb * 64, 64), 64)
                        for r in range(2):
                            at = (2 * dr + pa + 1 - r) * 8 + 2 * dt + pb
                            value = jnp.where(diag, taps[2 * k + g, pl.ds(at, 1), :], 0.0)
                            rhs[slot, g, dt, to, r * 128 : (r + 1) * 128] = value.astype(BF16)
            return 0

        lax.fori_loop(0, 16, weights, 0)

    def conv_at(g, a, first, count, stride=None):
        return pl.ds((2 * g + a) * NM + first, count, stride=stride)

    def convolve(blk, k):
        slot = (3 * blk + k) % 2

        def own(big, _):
            src = pl.ds(pl.multiple_of(big * NR, NR), NR)
            for a in range(2):
                for b in range(2):
                    value = state[k, 2 * a + b, src, :] * share[2 * a + b, src, :]
                    padded[2 * (1 - a) + 1 - b, pl.ds((big + 1 + b) * QR + 1 + a, NR), :] = value
            return 0

        lax.fori_loop(0, HALF, own, 0)
        arrived(sideways(blk, k))
        pl.when(has_north)(lambda: arrived(down(blk, k)))
        pl.when(has_south)(lambda: arrived(up(blk, k)))
        for side, places in enumerate((LOW, ROW_TOP)):
            for n, (pa, pr) in enumerate(places):
                for b in range(2):
                    padded[2 * pa + 1 - b, pl.ds((1 + b) * QR + pr, NT, stride=QR), :] = row_halo[
                        blk, k, side, n, b
                    ].astype(F32)
        for side, places in enumerate((LOW, COL_TOP)):
            for n, (pb, pt) in enumerate(places):
                for a in range(2):
                    at = pt * QR + 1 + a
                    padded[2 * (1 - a) + pb, at : at + NR, :] = col_halo[blk, k, side, n, a].astype(F32)
        for rside, rplaces in enumerate((LOW, ROW_TOP)):
            for cside, cplaces in enumerate((LOW, COL_TOP)):
                tmp[0:16, :] = corner_halo[blk, k, rside, cside].astype(F32)
                for n, (pa, pr) in enumerate(rplaces):
                    for m, (pb, pt) in enumerate(cplaces):
                        at = pt * QR + pr
                        padded[2 * pa + pb, at : at + 1, :] = tmp[3 * n + m : 3 * n + m + 1, :]

        def pair_up(big, _):
            at = pl.ds(pl.multiple_of(big * 8 * QR, 8 * QR), 8 * QR)
            low = lane_low((8 * QR, 128))
            for pa in range(2):
                even, odd = padded[2 * pa, at, :], padded[2 * pa + 1, at, :]
                paired[0, pa, at, :] = jnp.where(low, even, pltpu.roll(odd, 64, 1))
                paired[1, pa, at, :] = jnp.where(low, pltpu.roll(even, 64, 1), odd)
            return 0

        lax.fori_loop(0, NT // 8, pair_up, 0)

        def spread(big, _):
            to = pl.ds(pl.multiple_of(big * NR, NR), NR)
            for g in range(2):
                for d in range(4):
                    for pa in range(2):
                        c0 = d * 256 + pa * 128
                        lhs[g, to, c0 : c0 + 128] = paired[
                            g, pa, pl.ds(big * QR + d, NR), :
                        ].astype(BF16)
            return 0

        lax.fori_loop(0, NT, spread, 0)
        for g in range(2):
            total = None
            for d in range(4):
                part = jnp.dot(
                    lhs[g, d * NR : d * NR + USED, :], rhs[slot, g, d], preferred_element_type=F32
                )
                total = part if total is None else total + part
            for a in range(2):
                table[k, conv_at(g, a, 0, USED), :] = total[:, a * 128 : (a + 1) * 128]

    def conv_rows(a, first, count, stride=None):
        low = lane_low((count, 128))
        chunks = []
        for k in range(3):
            even = table[k, conv_at(0, a, first, count, stride), :]
            odd = table[k, conv_at(1, a, first, count, stride), :]
            chunks.append(
                [
                    jnp.where(low, even, pltpu.roll(odd, 64, 1)),
                    jnp.where(low, pltpu.roll(even, 64, 1), odd),
                ]
            )
        return chunks

    def feed(blk, chunks):
        centre = jnp.sum(chunks[0] + chunks[1] + chunks[2], axis=1, keepdims=True) * (1.0 / CH)
        chunks = [c - centre for c in chunks]
        squares = chunks[0] * chunks[0] + chunks[1] * chunks[1] + chunks[2] * chunks[2]
        scale = lax.rsqrt(jnp.sum(squares, axis=1, keepdims=True) * (1.0 / CH) + 1e-06)
        normed = jnp.concatenate(
            [
                (c * scale * gain[blk : blk + 1, k * 128 : (k + 1) * 128]).astype(BF16)
                for k, c in enumerate(chunks)
            ],
            axis=1,
        )
        update = None
        for f in range(0, FF, 512):
            u = jnp.dot(normed, expand[:, f : f + 512], preferred_element_type=F32)
            h = 0.5 * u
            t = jnp.tanh(u * (0.7978845608028654 + 0.035677408136300125 * (u * u)))
            part = jnp.dot(
                (h + h * t).astype(BF16), contract[f : f + 512, :], preferred_element_type=F32
            )
            update = part if update is None else update + part
        return update

    def mlp(blk):
        @pl.when(top)
        def _():
            for k in range(3):
                for s in range(1, 8):
                    ring_copy(blk, k, s).wait_recv()
                forward(blk, k).start()
                for i, (a, big) in enumerate(ROW_HIGH):
                    for b in range(2):
                        saved[k, i, b] = state[k, 2 * a + b, pl.ds(big, NT, stride=NR), :]

        for c in mlp_loads(blk):
            c.wait()
        tile = 240
        for a in range(2):
            for i in range(USED // tile):
                at = slice(i * tile, (i + 1) * tile)
                update = feed(blk, [jnp.concatenate(c, axis=0) for c in conv_rows(a, i * tile, tile)])
                for b in range(2):
                    for k in range(3):
                        state[k, 2 * a + b, at, :] += (
                            share[2 * a + b, at, :]
                            * update[b * tile : (b + 1) * tile, k * 128 : (k + 1) * 128]
                        )

        @pl.when(top)
        def _():
            first = lax.rem(fold[0] - 92 + NLON, NLON)
            sector = lax.div(first, COLS)
            off = first - sector * COLS
            at_out = lax.broadcasted_iota(jnp.int32, (2 * NT, 2 * NT), 0)
            at_in = lax.broadcasted_iota(jnp.int32, (2 * NT, 2 * NT), 1)
            wanted = off + 95 - jnp.where(at_out >= NT, 2 * (at_out - NT) + 1, 2 * at_out)
            pair = jnp.where(at_in >= NT, at_in - NT, at_in)
            column = 2 * pair + jnp.where(at_in >= NT, 1, 0)
            picked = [
                jnp.where((column + s * COLS == wanted) & (pair < HALF), 1.0, 0.0).astype(BF16)
                for s in range(3)
            ]
            low = lane_low((56, 128))
            for k in range(3):
                forward(blk, k).wait()
            for k in range(3):
                for n in range(3):
                    got = jnp.zeros((2 * NT, 128), F32)
                    for s in range(3):
                        source = lax.rem(sector + s, LONS)
                        strip = ring[blk][k, lax.rem(source, 2), lax.div(source, 2), 2 - n]
                        got += jnp.dot(
                            picked[s], strip.reshape(2 * NT, 128), preferred_element_type=F32
                        )
                    for pb in range(2):
                        tmp[0:NT, :] = got[pb * NT : (pb + 1) * NT]
                        tmp[NT:56, :] = jnp.zeros((8, 128), F32)
                        value = tmp[0:56, :]
                        turned = pltpu.roll(value, 64, 1)
                        folded[2 * k, n, pb] = jnp.where(low, value, turned)
                        folded[2 * k + 1, n, pb] = jnp.where(low, turned, value)

            def correct(k, _):
                for g in range(2):
                    for i, (a, big) in enumerate(ROW_HIGH):
                        at = conv_at(g, a, big, NT, NR)
                        total = table[k, at, :]
                        for n in range(i + 1):
                            row = 8 * (7 + n - i)
                            for e in range(8):
                                total += (
                                    folded[2 * k + g, n, e % 2, e // 2 : e // 2 + NT, :]
                                    * taps[2 * k + g, row + e : row + e + 1, :]
                                )
                        table[k, at, :] = total
                return 0

            lax.fori_loop(0, 3, correct, 0)
            rows = [conv_rows(a, big, NT, NR) for a, big in ROW_HIGH]
            update = feed(
                blk, [jnp.concatenate([r[k][b] for r in rows for b in range(2)], axis=0) for k in range(3)]
            )
            for i, (a, big) in enumerate(ROW_HIGH):
                for b in range(2):
                    at = pl.ds(big, NT, stride=NR)
                    part = update[(2 * i + b) * NT : (2 * i + b + 1) * NT]
                    for k in range(3):
                        state[k, 2 * a + b, at, :] = (
                            saved[k, i, b]
                            + share[2 * a + b, at, :] * part[:, k * 128 : (k + 1) * 128]
                        )

    def remap(k):
        for side in range(2):
            flux_copy(k, 1 - side).wait_recv()

            def widened(i, _, side=side):
                at = pl.multiple_of(i * 288, 288)
                table[k, pl.ds(3 * side * CELLS + at, 288), :] = incoming[
                    k, side, pl.ds(at, 288), :
                ].astype(F32)
                return 0

            lax.fori_loop(0, CELLS // 288, widened, 0)

        def gather_cells(big, _):
            base = pl.multiple_of(big * NR, NR)
            for a in range(2):
                for b in range(2):
                    for r in range(NR):
                        paired[a, b, pl.ds(base + r, 1), :] = table[
                            k, pl.ds(picks[2 * r + a, 2 * big + b], 1), :
                        ]
            return 0

        lax.fori_loop(0, HALF, gather_cells, 0)
        for a in range(2):
            for b in range(2):
                state[k, 2 * a + b, 0:USED, :] += paired[a, b, 0:USED, :]

    build_taps(0)
    build_weights(0, 0)
    build_weights(0, 1)
    remap(0)
    send_edges(0, 0)
    remap(1)
    send_edges(0, 1)
    convolve(0, 0)
    build_weights(0, 2)
    remap(2)
    send_edges(0, 2)
    convolve(0, 1)
    convolve(0, 2)
    mlp(0)
    start(mlp_loads(1))
    for k in range(3):
        edges_sent(0, k)
        send_edges(1, k)
    build_taps(1)
    build_weights(1, 0)
    build_weights(1, 1)
    convolve(1, 0)
    build_weights(1, 2)
    convolve(1, 1)
    convolve(1, 2)
    mlp(1)

    def natural(big, _):
        at = pl.ds(pl.multiple_of(big * NR, NR), NR)
        for b in range(2):
            for k in range(3):
                for a in range(2):
                    tmp[pl.ds(a, NR, stride=2), :] = state[k, 2 * a + b, at, :]
                out[2 * big + b, :, k * 128 : (k + 1) * 128] = tmp[0:ROWS, :].astype(BF16)
        return 0

    lax.fori_loop(0, HALF, natural, 0)
    for k in range(3):
        edges_sent(1, k)
        for side in range(2):
            flux_copy(k, side).wait_send()


def step(picks, sea_mask, fold, weight, taps, gain, atmos, ocean, expand, contract):
    vmem, smem = (pl.BlockSpec(memory_space=m) for m in (pltpu.VMEM, pltpu.SMEM))
    anywhere = pl.BlockSpec(memory_space=pl.ANY)
    edges = [(3, 2, 3, 2, NT, 128), (3, 2, 3, 2, NR, 128), (3, 2, 2, 16, 128)]
    return pl.pallas_call(
        ocean_kernel,
        out_shape=jax.ShapeDtypeStruct((COLS, ROWS, CH), BF16),
        in_specs=[smem] * 3 + [vmem] * 3 + [anywhere] * 4,
        out_specs=vmem,
        scratch_shapes=[
            pltpu.VMEM((2 * CELLS, CA), BF16),
            pltpu.VMEM((COLS, ROWS, CH), BF16),
            pltpu.VMEM((3, 4 * CELLS + 8, 128), F32),
            pltpu.VMEM((3, 2, CELLS, 128), BF16),
            pltpu.VMEM((3, 2, CELLS, 128), BF16),
            pltpu.VMEM((3, 4, NM, 128), F32),
            pltpu.VMEM((4, NM, 128), F32),
            *(pltpu.VMEM(e, BF16) for e in edges),
            *(pltpu.VMEM((2, *e), BF16) for e in edges),
            pltpu.VMEM((3, 2, LONS // 2, 3, 2, NT, 128), BF16),
            pltpu.VMEM((3, 2, LONS // 2, 3, 2, NT, 128), BF16),
            pltpu.VMEM((4, QR * QT, 128), F32),
            pltpu.VMEM((2, 2, QR * NT, 128), F32),
            pltpu.VMEM((2, NT * NR, 1024), BF16),
            pltpu.VMEM((2, 2, 4, 1024, 256), BF16),
            pltpu.VMEM((96, 128), F32),
            pltpu.VMEM((6, 72, 128), F32),
            pltpu.VMEM((6, 3, 2, 56, 128), F32),
            pltpu.VMEM((3, 3, 2, NT, 128), F32),
            pltpu.VMEM((CH, FF), BF16),
            pltpu.VMEM((FF, CH), BF16),
            pltpu.SemaphoreType.DMA((5,)),
            pltpu.SemaphoreType.DMA((3, 2)),
            pltpu.SemaphoreType.DMA((3, 2)),
            pltpu.SemaphoreType.DMA((2, 3, 8)),
            pltpu.SemaphoreType.DMA((2, 3, 8)),
            pltpu.SemaphoreType.DMA((2, 3, 8)),
            pltpu.SemaphoreType.DMA((2, 3, 8)),
        ],
        compiler_params=pltpu.CompilerParams(
            collective_id=0, has_side_effects=True, vmem_limit_bytes=VLIMIT
        ),
    )(picks, sea_mask, fold, weight, taps, gain, atmos, ocean, expand, contract)


def body(atmos, ocean, remap, fold, sea_mask, flux_weight, dw_kernel, norm_gain, w_in, w_out):
    band = lax.axis_index(("sec", "lat"))
    lon = lax.axis_index("lon")
    row = remap // NLON
    col = (remap - row * NLON - lon * COLS + HALF + NLON) % NLON
    picks = jnp.where(sea_mask == 0, 4 * CELLS, col * ROWS + row - band * ROWS)
    atmos = atmos.transpose(1, 0, 2).reshape(COLS * ROWS, CA)
    ocean = ocean.transpose(1, 0, 2)
    taps = dw_kernel.transpose(1, 2, 0, 3)
    out = step(picks, sea_mask, fold, flux_weight, taps, norm_gain, atmos, ocean, w_in, w_out)
    return out.transpose(1, 0, 2)


def solution(mesh):
    return jax.shard_map(
        body,
        mesh=mesh,
        in_specs=(
            P(("sec", "lat"), "lon", None),
            P(("sec", "lat"), "lon", None),
            P(("sec", "lat"), "lon"),
            P("lon"),
            P(("sec", "lat"), "lon"),
            P(),
            P(),
            P(),
            P(),
            P(),
        ),
        out_specs=P(("sec", "lat"), "lon", None),
        check_vma=False,
    )
```

```python
import jax
import jax.numpy as jnp
from jax import lax
from jax.experimental import pallas as pl
from jax.experimental.pallas import tpu as pltpu
from jax.sharding import PartitionSpec as P

ROWS, COLS, CH, CA, FF = 32, 90, 384, 512, 1536
HALF = 45
CELLS = ROWS * HALF
BANDS, LONS = 8, 16
NLON = COLS * LONS
NR, NT, NM, USED = 16, 48, 768, 720
QR, QT = 24, 50
LOW = ((0, 0), (1, 0), (0, 1))
ROW_HIGH = ((1, 14), (0, 15), (1, 15))
COL_HIGH = ((1, 43), (0, 44), (1, 44))
ROW_TOP = ((1, 17), (0, 18), (1, 18))
COL_TOP = ((1, 46), (0, 47), (1, 47))
MESH = pl.DeviceIdType.MESH
F32, BF16 = jnp.float32, jnp.bfloat16
VLIMIT = 60 * 2**20


def lane_low(shape):
    return lax.broadcasted_iota(jnp.int32, shape, len(shape) - 1) < 64


def ocean_kernel(
    picks, sea, fold, weight, kernel_taps, gain, atmos_in, ocean_in, expand_all, contract_all,
    out,
    atmos, ocean, table, outgoing, incoming, state, share, row_out, col_out, corner_out, row_halo, col_halo, corner_halo,
    ring_00, ring_01, ring_02, ring_10, ring_11, ring_12, padded, paired, lhs, rhs, tmp, taps, folded, expand, contract,
    load_sem, flux_send, flux_recv, halo_send, halo_recv, ring_send, ring_recv,
):
    ring = ((ring_00, ring_01, ring_02), (ring_10, ring_11, ring_12))

    def load(n, src, dst):
        return pltpu.make_async_copy(src, dst, load_sem.at[n])

    atmos_loads = [
        load(side, atmos_in.at[pl.ds(side * CELLS, CELLS)], atmos.at[pl.ds(side * CELLS, CELLS)])
        for side in range(2)
    ]
    ocean_load = load(2, ocean_in, ocean)

    def mlp_loads(blk):
        return [load(3, expand_all.at[blk], expand), load(4, contract_all.at[blk], contract)]

    def start(copies):
        for c in copies:
            c.start()

    def arrived(copies):
        for c in copies:
            c.wait_recv()

    def sent(copies):
        for c in copies:
            c.wait_send()

    start(atmos_loads)
    ocean_load.start()
    start(mlp_loads(0))

    sec, lat, lon = (lax.axis_index(n) for n in ("sec", "lat", "lon"))
    band = sec * 4 + lat
    chip, core = lon // 2, lax.rem(lon, 2)
    sibling = lon + 1 - 2 * core
    left, right = lax.rem(lon + LONS - 1, LONS), lax.rem(lon + 1, LONS)
    has_north, has_south, top = band < BANDS - 1, band > 0, band == BANDS - 1

    def place(step, where):
        other = band + step
        return (other // 4, lax.rem(other, 4), where)

    def peer(step):
        return (sec, lat, lax.rem(lon + 2 * step, LONS))

    barrier = pltpu.get_barrier_semaphore()

    def greet(device):
        pl.semaphore_signal(barrier, inc=1, device_id=device, device_id_type=MESH)

    greet((sec, lat, left))
    greet((sec, lat, right))
    pl.when(has_north)(lambda: [greet(place(1, w)) for w in (left, lon, right)] and None)
    pl.when(has_south)(lambda: [greet(place(-1, w)) for w in (left, lon, right)] and None)
    pl.when(top)(lambda: [greet(peer(s)) for s in range(1, 8)] and None)
    greeted = 2 + jnp.where(has_north, 3, 0) + jnp.where(has_south, 3, 0) + jnp.where(top, 7, 0)
    pl.semaphore_wait(barrier, greeted)

    def flux_copy(k, side):
        return pltpu.make_async_remote_copy(
            src_ref=outgoing.at[k, side], dst_ref=incoming.at[k, 1 - side],
            send_sem=flux_send.at[k, side], recv_sem=flux_recv.at[k, 1 - side],
            device_id=(sec, lat, (left, right)[side]), device_id_type=MESH,
        )

    for k in range(3):
        for side in range(2):
            if k == 0:
                atmos_loads[side].wait()

            def cells(i, _, k=k, side=side):
                at = pl.multiple_of(i * 288, 288)
                value = jnp.dot(
                    atmos[pl.ds(side * CELLS + at, 288), :],
                    weight[:, k * 128 : (k + 1) * 128],
                    preferred_element_type=F32,
                ).astype(BF16)
                outgoing[k, side, pl.ds(at, 288), :] = value
                table[k, pl.ds((1 + side) * CELLS + at, 288), :] = value.astype(F32)
                return 0

            lax.fori_loop(0, CELLS // 288, cells, 0)
            flux_copy(k, side).start()
        table[k, 4 * CELLS : 4 * CELLS + 8, :] = jnp.zeros((8, 128), F32)

    for q in range(4):
        share[q, USED:NM, :] = jnp.zeros((NM - USED, 128), F32)
        for k in range(3):
            state[k, q, USED:NM, :] = jnp.zeros((NM - USED, 128), F32)
    tmp[0:16, :] = jnp.zeros((16, 128), F32)
    tmp[1:2, :] = jnp.ones((1, 128), F32)

    def share_cells(big, _):
        base = pl.multiple_of(big * NR, NR)
        for a in range(2):
            for b in range(2):
                for r in range(NR):
                    share[2 * a + b, pl.ds(base + r, 1), :] = tmp[
                        pl.ds(sea[2 * r + a, 2 * big + b], 1), :
                    ]
        return 0

    lax.fori_loop(0, HALF, share_cells, 0)
    ocean_load.wait()

    def ocean_cells(big, _):
        at = pl.ds(pl.multiple_of(big * NR, NR), NR)
        for b in range(2):
            for k in range(3):
                own = (3 * b + k) * ROWS
                tmp[own : own + ROWS, :] = ocean[2 * big + b, :, k * 128 : (k + 1) * 128].astype(F32)
                for a in range(2):
                    state[k, 2 * a + b, at, :] = tmp[pl.ds(own + a, NR, stride=2), :]
        return 0

    lax.fori_loop(0, HALF, ocean_cells, 0)
    padded[...] = jnp.zeros_like(padded)

    @pl.when(jnp.logical_not(has_south))
    def _():
        for blk in range(2):
            row_halo[blk, :, 0] = jnp.zeros((3, *row_halo.shape[3:]), BF16)
            corner_halo[blk, :, 0] = jnp.zeros((3, *corner_halo.shape[3:]), BF16)

    @pl.when(top)
    def _():
        for blk in range(2):
            row_halo[blk, :, 1] = jnp.zeros((3, *row_halo.shape[3:]), BF16)
            corner_halo[blk, :, 1] = jnp.zeros((3, *corner_halo.shape[3:]), BF16)

    def copy(blk, k, n, src, dst, device):
        return pltpu.make_async_remote_copy(
            src_ref=src, dst_ref=dst, send_sem=halo_send.at[blk, k, n], recv_sem=halo_recv.at[blk, k, n],
            device_id=device, device_id_type=MESH,
        )

    def sideways(blk, k):
        return [
            copy(blk, k, 0, col_out.at[k, 1], col_halo.at[blk, k, 0], (sec, lat, right)),
            copy(blk, k, 1, col_out.at[k, 0], col_halo.at[blk, k, 1], (sec, lat, left)),
        ]

    def up(blk, k):
        return [
            copy(blk, k, 2, row_out.at[k, 1], row_halo.at[blk, k, 0], place(1, lon)),
            copy(blk, k, 3, corner_out.at[k, 1, 0], corner_halo.at[blk, k, 0, 1], place(1, left)),
            copy(blk, k, 4, corner_out.at[k, 1, 1], corner_halo.at[blk, k, 0, 0], place(1, right)),
        ]

    def down(blk, k):
        return [
            copy(blk, k, 5, row_out.at[k, 0], row_halo.at[blk, k, 1], place(-1, lon)),
            copy(blk, k, 6, corner_out.at[k, 0, 0], corner_halo.at[blk, k, 1, 1], place(-1, left)),
            copy(blk, k, 7, corner_out.at[k, 0, 1], corner_halo.at[blk, k, 1, 0], place(-1, right)),
        ]

    def ring_copy(blk, k, step):
        return pltpu.make_async_remote_copy(
            src_ref=row_out.at[k, 1], dst_ref=ring[blk][k].at[core, chip],
            send_sem=ring_send.at[blk, k, step], recv_sem=ring_recv.at[blk, k, step],
            device_id=peer(step), device_id_type=MESH,
        )

    def forward(blk, k):
        return pltpu.make_async_remote_copy(
            src_ref=ring[blk][k].at[core], dst_ref=ring[blk][k].at[core],
            send_sem=ring_send.at[blk, k, 0], recv_sem=ring_recv.at[blk, k, 0],
            device_id=(sec, lat, sibling), device_id_type=MESH,
        )

    def send_edges(blk, k):
        for side, edge in enumerate((LOW, COL_HIGH)):
            for n, (b, big) in enumerate(edge):
                for a in range(2):
                    at = slice(big * NR, (big + 1) * NR)
                    col_out[k, side, n, a] = (
                        state[k, 2 * a + b, at, :] * share[2 * a + b, at, :]
                    ).astype(BF16)
        for side, edge in enumerate((LOW, ROW_HIGH)):
            for n, (a, big) in enumerate(edge):
                for b in range(2):
                    at = pl.ds(big, NT, stride=NR)
                    row_out[k, side, n, b] = (
                        state[k, 2 * a + b, at, :] * share[2 * a + b, at, :]
                    ).astype(BF16)
        tmp[9:16, :] = jnp.zeros((7, 128), F32)
        for rside, redge in enumerate((LOW, ROW_HIGH)):
            for cside, cedge in enumerate((LOW, COL_HIGH)):
                for n, (a, rbig) in enumerate(redge):
                    for m, (b, cbig) in enumerate(cedge):
                        at = slice(cbig * NR + rbig, cbig * NR + rbig + 1)
                        tmp[3 * n + m : 3 * n + m + 1, :] = (
                            state[k, 2 * a + b, at, :] * share[2 * a + b, at, :]
                        )
                corner_out[k, rside, cside] = tmp[0:16, :].astype(BF16)
        start(sideways(blk, k))
        pl.when(has_north)(lambda: start(up(blk, k)))
        pl.when(has_south)(lambda: start(down(blk, k)))

        @pl.when(top)
        def _():
            start([ring_copy(blk, k, s) for s in (4, 3, 5, 2, 6, 1, 7)])
            ring[blk][k][core, chip] = row_out[k, 1]

    def edges_sent(blk, k):
        sent(sideways(blk, k))
        pl.when(has_north)(lambda: sent(up(blk, k)))
        pl.when(has_south)(lambda: sent(down(blk, k)))
        pl.when(top)(lambda: sent([ring_copy(blk, k, s) for s in range(1, 8)]))

    def build_taps(blk):
        taps[...] = jnp.zeros_like(taps)
        tmp[0:16, :] = jnp.zeros((16, 128), F32)
        low = lane_low((8, 128))
        for row in range(7):
            for k in range(3):
                for e in range(7):
                    tmp[1 + e : 2 + e, :] = kernel_taps[row, e, blk : blk + 1, k * 128 : (k + 1) * 128]
                now, before = tmp[1:9, :], tmp[0:8, :]
                at = slice(8 * (row + 1), 8 * (row + 2))
                taps[2 * k, at, :] = jnp.where(low, now, pltpu.roll(before, 64, 1))
                taps[2 * k + 1, at, :] = jnp.where(low, pltpu.roll(now, 64, 1), before)

    def build_weights(blk, k):
        slot = (3 * blk + k) % 2

        def weights(i, _):
            dr, dt = i // 4, lax.rem(i, 4)
            diag = (
                lax.broadcasted_iota(jnp.int32, (64, 128), 0)
                == lax.broadcasted_iota(jnp.int32, (64, 128), 1) % 64
            )
            for g in range(2):
                for pa in range(2):
                    for pb in range(2):
                        to = pl.ds(pl.multiple_of(dr * 256 + pa * 128 + pb * 64, 64), 64)
                        for r in range(2):
                            at = (2 * dr + pa + 1 - r) * 8 + 2 * dt + pb
                            value = jnp.where(diag, taps[2 * k + g, pl.ds(at, 1), :], 0.0)
                            rhs[slot, g, dt, to, r * 128 : (r + 1) * 128] = value.astype(BF16)
            return 0

        lax.fori_loop(0, 16, weights, 0)

    def conv_at(g, a, first, count, stride=None):
        return pl.ds((2 * g + a) * NM + first, count, stride=stride)

    def convolve(blk, k):
        slot = (3 * blk + k) % 2

        def own(i, _):
            for j in range(5):
                big = 5 * i + j
                src = pl.ds(pl.multiple_of(big * NR, NR), NR)
                for a in range(2):
                    for b in range(2):
                        value = state[k, 2 * a + b, src, :] * share[2 * a + b, src, :]
                        padded[2 * (1 - a) + 1 - b, pl.ds((big + 1 + b) * QR + 1 + a, NR), :] = value
            return 0

        lax.fori_loop(0, HALF // 5, own, 0)
        arrived(sideways(blk, k))
        pl.when(has_north)(lambda: arrived(down(blk, k)))
        pl.when(has_south)(lambda: arrived(up(blk, k)))
        for side, places in enumerate((LOW, ROW_TOP)):
            for n, (pa, pr) in enumerate(places):
                for b in range(2):
                    padded[2 * pa + 1 - b, pl.ds((1 + b) * QR + pr, NT, stride=QR), :] = row_halo[
                        blk, k, side, n, b
                    ].astype(F32)
        for side, places in enumerate((LOW, COL_TOP)):
            for n, (pb, pt) in enumerate(places):
                for a in range(2):
                    at = pt * QR + 1 + a
                    padded[2 * (1 - a) + pb, at : at + NR, :] = col_halo[blk, k, side, n, a].astype(F32)
        for rside, rplaces in enumerate((LOW, ROW_TOP)):
            for cside, cplaces in enumerate((LOW, COL_TOP)):
                tmp[0:16, :] = corner_halo[blk, k, rside, cside].astype(F32)
                for n, (pa, pr) in enumerate(rplaces):
                    for m, (pb, pt) in enumerate(cplaces):
                        at = pt * QR + pr
                        padded[2 * pa + pb, at : at + 1, :] = tmp[3 * n + m : 3 * n + m + 1, :]

        def pair_up(big, _):
            at = pl.ds(pl.multiple_of(big * 8 * QR, 8 * QR), 8 * QR)
            low = lane_low((8 * QR, 128))
            for pa in range(2):
                even, odd = padded[2 * pa, at, :], padded[2 * pa + 1, at, :]
                paired[0, pa, at, :] = jnp.where(low, even, pltpu.roll(odd, 64, 1))
                paired[1, pa, at, :] = jnp.where(low, pltpu.roll(even, 64, 1), odd)
            return 0

        lax.fori_loop(0, NT // 8, pair_up, 0)

        def spread(i, _):
            for j in range(4):
                big = 4 * i + j
                to = pl.ds(pl.multiple_of(big * NR, NR), NR)
                for g in range(2):
                    for d in range(4):
                        for pa in range(2):
                            c0 = d * 256 + pa * 128
                            lhs[g, to, c0 : c0 + 128] = paired[
                                g, pa, pl.ds(big * QR + d, NR), :
                            ].astype(BF16)
            return 0

        lax.fori_loop(0, NT // 4, spread, 0)
        for g in range(2):
            total = None
            for d in range(4):
                part = jnp.dot(
                    lhs[g, d * NR : d * NR + USED, :], rhs[slot, g, d], preferred_element_type=F32
                )
                total = part if total is None else total + part
            for a in range(2):
                table[k, conv_at(g, a, 0, USED), :] = total[:, a * 128 : (a + 1) * 128]

    def conv_rows(a, first, count, stride=None):
        low = lane_low((count, 128))
        chunks = []
        for k in range(3):
            even = table[k, conv_at(0, a, first, count, stride), :]
            odd = table[k, conv_at(1, a, first, count, stride), :]
            chunks.append(
                [
                    jnp.where(low, even, pltpu.roll(odd, 64, 1)),
                    jnp.where(low, pltpu.roll(even, 64, 1), odd),
                ]
            )
        return chunks

    def feed(blk, chunks):
        centre = jnp.sum(chunks[0] + chunks[1] + chunks[2], axis=1, keepdims=True) * (1.0 / CH)
        chunks = [c - centre for c in chunks]
        squares = chunks[0] * chunks[0] + chunks[1] * chunks[1] + chunks[2] * chunks[2]
        scale = lax.rsqrt(jnp.sum(squares, axis=1, keepdims=True) * (1.0 / CH) + 1e-06)
        normed = jnp.concatenate(
            [
                (c * scale * gain[blk : blk + 1, k * 128 : (k + 1) * 128]).astype(BF16)
                for k, c in enumerate(chunks)
            ],
            axis=1,
        )
        update = None
        for f in range(0, FF, 512):
            u = jnp.dot(normed, expand[:, f : f + 512], preferred_element_type=F32)
            h = 0.5 * u
            t = jnp.tanh(u * (0.7978845608028654 + 0.035677408136300125 * (u * u)))
            part = jnp.dot(
                (h + h * t).astype(BF16), contract[f : f + 512, :], preferred_element_type=F32
            )
            update = part if update is None else update + part
        return update

    def pass_on(blk, k):
        @pl.when(top)
        def _():
            for s in range(1, 8):
                ring_copy(blk, k, s).wait_recv()
            forward(blk, k).start()

    def fold_in(blk, k):
        @pl.when(top)
        def _():
            forward(blk, k).wait()
            first = lax.rem(fold[0] - 92 + NLON, NLON)
            sector = lax.div(first, COLS)
            off = first - sector * COLS
            at_out = lax.broadcasted_iota(jnp.int32, (2 * NT, 2 * NT), 0)
            at_in = lax.broadcasted_iota(jnp.int32, (2 * NT, 2 * NT), 1)
            wanted = off + 95 - jnp.where(at_out >= NT, 2 * (at_out - NT) + 1, 2 * at_out)
            pair = jnp.where(at_in >= NT, at_in - NT, at_in)
            column = 2 * pair + jnp.where(at_in >= NT, 1, 0)
            got = jnp.zeros((2 * NT, CH), F32)
            for s in range(3):
                source = lax.rem(sector + s, LONS)
                picked = jnp.where((column + s * COLS == wanted) & (pair < HALF), 1.0, 0.0).astype(BF16)
                strip = ring[blk][k][lax.rem(source, 2), lax.div(source, 2)]
                rows = [strip[2 - n].reshape(2 * NT, 128) for n in range(3)]
                got += jnp.dot(picked, jnp.concatenate(rows, axis=1), preferred_element_type=F32)
            low = lane_low((56, 128))
            for n in range(3):
                for pb in range(2):
                    at = (2 * n + pb) * 64
                    tmp[at : at + NT, :] = got[pb * NT : (pb + 1) * NT, n * 128 : (n + 1) * 128]
                    tmp[at + NT : at + 56, :] = jnp.zeros((8, 128), F32)
                    value = tmp[at : at + 56, :]
                    turned = pltpu.roll(value, 64, 1)
                    folded[0, n, pb] = jnp.where(low, value, turned)
                    folded[1, n, pb] = jnp.where(low, turned, value)
            for g in range(2):
                for i, (a, big) in enumerate(ROW_HIGH):
                    at = conv_at(g, a, big, NT, NR)
                    total = table[k, at, :]
                    for n in range(i + 1):
                        row = 8 * (7 + n - i)
                        for e in range(8):
                            total += (
                                folded[g, n, e % 2, e // 2 : e // 2 + NT, :]
                                * taps[2 * k + g, row + e : row + e + 1, :]
                            )
                    table[k, at, :] = total

    def mlp(blk):
        for c in mlp_loads(blk):
            c.wait()
        tile = 240
        for a in range(2):
            for i in range(USED // tile):
                at = slice(i * tile, (i + 1) * tile)
                update = feed(blk, [jnp.concatenate(c, axis=0) for c in conv_rows(a, i * tile, tile)])
                for b in range(2):
                    for k in range(3):
                        state[k, 2 * a + b, at, :] += (
                            share[2 * a + b, at, :]
                            * update[b * tile : (b + 1) * tile, k * 128 : (k + 1) * 128]
                        )

    def remap(k):
        for side in range(2):
            flux_copy(k, 1 - side).wait_recv()

            def widened(i, _, side=side):
                at = pl.multiple_of(i * 288, 288)
                table[k, pl.ds(3 * side * CELLS + at, 288), :] = incoming[
                    k, side, pl.ds(at, 288), :
                ].astype(F32)
                return 0

            lax.fori_loop(0, CELLS // 288, widened, 0)

        def gather_cells(big, _):
            base = pl.multiple_of(big * NR, NR)
            for a in range(2):
                for b in range(2):
                    for r in range(NR):
                        paired[a, b, pl.ds(base + r, 1), :] = table[
                            k, pl.ds(picks[2 * r + a, 2 * big + b], 1), :
                        ]
            return 0

        lax.fori_loop(0, HALF, gather_cells, 0)
        for a in range(2):
            for b in range(2):
                state[k, 2 * a + b, 0:USED, :] += paired[a, b, 0:USED, :]

    build_taps(0)
    build_weights(0, 0)
    remap(0)
    send_edges(0, 0)
    build_weights(0, 1)
    convolve(0, 0)
    remap(1)
    send_edges(0, 1)
    build_weights(0, 2)
    pass_on(0, 0)
    convolve(0, 1)
    remap(2)
    send_edges(0, 2)
    fold_in(0, 0)
    pass_on(0, 1)
    convolve(0, 2)
    pass_on(0, 2)
    fold_in(0, 1)
    fold_in(0, 2)
    mlp(0)
    start(mlp_loads(1))
    for k in range(3):
        edges_sent(0, k)
        send_edges(1, k)
    build_taps(1)
    build_weights(1, 0)
    build_weights(1, 1)
    convolve(1, 0)
    build_weights(1, 2)
    pass_on(1, 0)
    convolve(1, 1)
    pass_on(1, 1)
    fold_in(1, 0)
    convolve(1, 2)
    pass_on(1, 2)
    fold_in(1, 1)
    fold_in(1, 2)
    mlp(1)

    def natural(i, _):
        for j in range(3):
            big = 3 * i + j
            at = pl.ds(pl.multiple_of(big * NR, NR), NR)
            for b in range(2):
                for k in range(3):
                    own = ((j * 2 + b) * 3 + k) * ROWS
                    for a in range(2):
                        tmp[pl.ds(own + a, NR, stride=2), :] = state[k, 2 * a + b, at, :]
                    out[2 * big + b, :, k * 128 : (k + 1) * 128] = tmp[own : own + ROWS, :].astype(BF16)
        return 0

    lax.fori_loop(0, HALF // 3, natural, 0)
    for k in range(3):
        edges_sent(1, k)
        for side in range(2):
            flux_copy(k, side).wait_send()


def step(picks, sea_mask, fold, weight, taps, gain, atmos, ocean, expand, contract):
    vmem, smem = (pl.BlockSpec(memory_space=m) for m in (pltpu.VMEM, pltpu.SMEM))
    anywhere = pl.BlockSpec(memory_space=pl.ANY)
    edges = [(3, 2, 3, 2, NT, 128), (3, 2, 3, 2, NR, 128), (3, 2, 2, 16, 128)]
    return pl.pallas_call(
        ocean_kernel,
        out_shape=jax.ShapeDtypeStruct((COLS, ROWS, CH), BF16),
        in_specs=[smem] * 3 + [vmem] * 3 + [anywhere] * 4,
        out_specs=vmem,
        scratch_shapes=[
            pltpu.VMEM((2 * CELLS, CA), BF16),
            pltpu.VMEM((COLS, ROWS, CH), BF16),
            pltpu.VMEM((3, 4 * CELLS + 8, 128), F32),
            pltpu.VMEM((3, 2, CELLS, 128), BF16),
            pltpu.VMEM((3, 2, CELLS, 128), BF16),
            pltpu.VMEM((3, 4, NM, 128), F32),
            pltpu.VMEM((4, NM, 128), F32),
            *(pltpu.VMEM(e, BF16) for e in edges),
            *(pltpu.VMEM((2, *e), BF16) for e in edges),
            *(pltpu.VMEM((2, LONS // 2, 3, 2, NT, 128), BF16) for _ in range(6)),
            pltpu.VMEM((4, QR * QT, 128), F32),
            pltpu.VMEM((2, 2, QR * NT, 128), F32),
            pltpu.VMEM((2, NT * NR, 1024), BF16),
            pltpu.VMEM((2, 2, 4, 1024, 256), BF16),
            pltpu.VMEM((18 * ROWS, 128), F32),
            pltpu.VMEM((6, 72, 128), F32),
            pltpu.VMEM((2, 3, 2, 56, 128), F32),
            pltpu.VMEM((CH, FF), BF16),
            pltpu.VMEM((FF, CH), BF16),
            pltpu.SemaphoreType.DMA((5,)),
            pltpu.SemaphoreType.DMA((3, 2)),
            pltpu.SemaphoreType.DMA((3, 2)),
            pltpu.SemaphoreType.DMA((2, 3, 8)),
            pltpu.SemaphoreType.DMA((2, 3, 8)),
            pltpu.SemaphoreType.DMA((2, 3, 8)),
            pltpu.SemaphoreType.DMA((2, 3, 8)),
        ],
        compiler_params=pltpu.CompilerParams(
            collective_id=0, has_side_effects=True, vmem_limit_bytes=VLIMIT
        ),
    )(picks, sea_mask, fold, weight, taps, gain, atmos, ocean, expand, contract)


def body(atmos, ocean, remap, fold, sea_mask, flux_weight, dw_kernel, norm_gain, w_in, w_out):
    band = lax.axis_index(("sec", "lat"))
    lon = lax.axis_index("lon")
    row = remap // NLON
    col = (remap - row * NLON - lon * COLS + HALF + NLON) % NLON
    picks = jnp.where(sea_mask == 0, 4 * CELLS, col * ROWS + row - band * ROWS)
    atmos = atmos.transpose(1, 0, 2).reshape(COLS * ROWS, CA)
    ocean = ocean.transpose(1, 0, 2)
    taps = dw_kernel.transpose(1, 2, 0, 3)
    out = step(picks, sea_mask, fold, flux_weight, taps, norm_gain, atmos, ocean, w_in, w_out)
    return out.transpose(1, 0, 2)


def solution(mesh):
    return jax.shard_map(
        body,
        mesh=mesh,
        in_specs=(
            P(("sec", "lat"), "lon", None),
            P(("sec", "lat"), "lon", None),
            P(("sec", "lat"), "lon"),
            P("lon"),
            P(("sec", "lat"), "lon"),
            P(),
            P(),
            P(),
            P(),
            P(),
        ),
        out_specs=P(("sec", "lat"), "lon", None),
        check_vma=False,
    )
```

```python
import jax
import jax.numpy as jnp
from jax import lax
from jax.experimental import pallas as pl
from jax.experimental.pallas import tpu as pltpu
from jax.sharding import PartitionSpec as P

ROWS, COLS, CH, CA, FF = 32, 90, 384, 512, 1536
HALF = 45
CELLS = ROWS * HALF
BANDS, LONS = 8, 16
NLON = COLS * LONS
NR, NT, NM, USED = 16, 48, 768, 720
QR, QT = 24, 50
LOW = ((0, 0), (1, 0), (0, 1))
ROW_HIGH = ((1, 14), (0, 15), (1, 15))
COL_HIGH = ((1, 43), (0, 44), (1, 44))
ROW_TOP = ((1, 17), (0, 18), (1, 18))
COL_TOP = ((1, 46), (0, 47), (1, 47))
MESH = pl.DeviceIdType.MESH
F32, BF16 = jnp.float32, jnp.bfloat16
VLIMIT = 60 * 2**20
PIECE = 1536


def lane_low(shape):
    return lax.broadcasted_iota(jnp.int32, shape, len(shape) - 1) < 64


def ocean_kernel(
    picks, sea, fold, weight, kernel_taps, gain, atmos_in, ocean_in, expand_all, contract_all,
    out,
    atmos, ocean, table, outgoing, incoming, state, share, row_out, col_out, corner_out, row_halo, col_halo, corner_halo,
    ring_00, ring_01, ring_02, ring_10, ring_11, ring_12, padded, paired, lhs, rhs, tmp, taps, folded, expand, contract,
    load_sem, flux_send, flux_recv, halo_send, halo_recv, ring_send, ring_recv,
):
    ring = ((ring_00, ring_01, ring_02), (ring_10, ring_11, ring_12))

    def load(n, src, dst):
        return pltpu.make_async_copy(src, dst, load_sem.at[n])

    atmos_loads = [
        load(side, atmos_in.at[pl.ds(side * CELLS, CELLS)], atmos.at[pl.ds(side * CELLS, CELLS)])
        for side in range(2)
    ]
    ocean_load = load(2, ocean_in, ocean)

    def mlp_loads(blk):
        return [load(3, expand_all.at[blk], expand), load(4, contract_all.at[blk], contract)]

    def start(copies):
        for c in copies:
            c.start()

    def arrived(copies):
        for c in copies:
            c.wait_recv()

    def sent(copies):
        for c in copies:
            c.wait_send()

    start(atmos_loads)
    ocean_load.start()
    start(mlp_loads(0))

    sec, lat, lon = (lax.axis_index(n) for n in ("sec", "lat", "lon"))
    band = sec * 4 + lat
    chip, core = lon // 2, lax.rem(lon, 2)
    sibling = lon + 1 - 2 * core
    left, right = lax.rem(lon + LONS - 1, LONS), lax.rem(lon + 1, LONS)
    has_north, has_south, top = band < BANDS - 1, band > 0, band == BANDS - 1

    def place(step, where):
        other = band + step
        return (other // 4, lax.rem(other, 4), where)

    def peer(step):
        return (sec, lat, lax.rem(lon + 2 * step, LONS))

    barrier = pltpu.get_barrier_semaphore()

    def greet(device):
        pl.semaphore_signal(barrier, inc=1, device_id=device, device_id_type=MESH)

    greet((sec, lat, left))
    greet((sec, lat, right))
    pl.when(has_north)(lambda: [greet(place(1, w)) for w in (left, lon, right)] and None)
    pl.when(has_south)(lambda: [greet(place(-1, w)) for w in (left, lon, right)] and None)
    pl.when(top)(lambda: [greet(peer(s)) for s in range(1, 8)] and None)
    greeted = 2 + jnp.where(has_north, 3, 0) + jnp.where(has_south, 3, 0) + jnp.where(top, 7, 0)
    pl.semaphore_wait(barrier, greeted)

    def flux_copy(k, side):
        return pltpu.make_async_remote_copy(
            src_ref=outgoing.at[k, side], dst_ref=incoming.at[k, 1 - side],
            send_sem=flux_send.at[k, side], recv_sem=flux_recv.at[k, 1 - side],
            device_id=(sec, lat, (left, right)[side]), device_id_type=MESH,
        )

    for k in range(3):
        for side in range(2):
            if k == 0:
                atmos_loads[side].wait()

            def cells(i, _, k=k, side=side):
                at = pl.multiple_of(i * 288, 288)
                value = jnp.dot(
                    atmos[pl.ds(side * CELLS + at, 288), :],
                    weight[:, k * 128 : (k + 1) * 128],
                    preferred_element_type=F32,
                ).astype(BF16)
                outgoing[k, side, pl.ds(at, 288), :] = value
                table[k, pl.ds((1 + side) * CELLS + at, 288), :] = value.astype(F32)
                return 0

            lax.fori_loop(0, CELLS // 288, cells, 0)
            if k < 2:
                flux_copy(k, side).start()
        table[k, 4 * CELLS : 4 * CELLS + 8, :] = jnp.zeros((8, 128), F32)

    for q in range(4):
        share[q, USED:NM, :] = jnp.zeros((NM - USED, 128), F32)
        for k in range(3):
            state[k, q, USED:NM, :] = jnp.zeros((NM - USED, 128), F32)
    tmp[0:16, :] = jnp.zeros((16, 128), F32)
    tmp[1:2, :] = jnp.ones((1, 128), F32)

    def share_cells(big, _):
        base = pl.multiple_of(big * NR, NR)
        for a in range(2):
            for b in range(2):
                for r in range(NR):
                    share[2 * a + b, pl.ds(base + r, 1), :] = tmp[
                        pl.ds(sea[2 * r + a, 2 * big + b], 1), :
                    ]
        return 0

    lax.fori_loop(0, HALF, share_cells, 0)
    ocean_load.wait()

    def ocean_cells(big, _):
        at = pl.ds(pl.multiple_of(big * NR, NR), NR)
        for b in range(2):
            for k in range(3):
                own = (3 * b + k) * ROWS
                tmp[own : own + ROWS, :] = ocean[2 * big + b, :, k * 128 : (k + 1) * 128].astype(F32)
                for a in range(2):
                    state[k, 2 * a + b, at, :] = tmp[pl.ds(own + a, NR, stride=2), :]
        return 0

    lax.fori_loop(0, HALF, ocean_cells, 0)
    padded[...] = jnp.zeros_like(padded)

    @pl.when(jnp.logical_not(has_south))
    def _():
        for blk in range(2):
            row_halo[blk, :, 0] = jnp.zeros((3, *row_halo.shape[3:]), BF16)
            corner_halo[blk, :, 0] = jnp.zeros((3, *corner_halo.shape[3:]), BF16)

    @pl.when(top)
    def _():
        for blk in range(2):
            row_halo[blk, :, 1] = jnp.zeros((3, *row_halo.shape[3:]), BF16)
            corner_halo[blk, :, 1] = jnp.zeros((3, *corner_halo.shape[3:]), BF16)

    def copy(blk, k, n, src, dst, device):
        return pltpu.make_async_remote_copy(
            src_ref=src, dst_ref=dst, send_sem=halo_send.at[blk, k, n], recv_sem=halo_recv.at[blk, k, n],
            device_id=device, device_id_type=MESH,
        )

    def sideways(blk, k):
        return [
            copy(blk, k, 0, col_out.at[k, 1], col_halo.at[blk, k, 0], (sec, lat, right)),
            copy(blk, k, 1, col_out.at[k, 0], col_halo.at[blk, k, 1], (sec, lat, left)),
        ]

    def up(blk, k):
        return [
            copy(blk, k, 2, row_out.at[k, 1], row_halo.at[blk, k, 0], place(1, lon)),
            copy(blk, k, 3, corner_out.at[k, 1, 0], corner_halo.at[blk, k, 0, 1], place(1, left)),
            copy(blk, k, 4, corner_out.at[k, 1, 1], corner_halo.at[blk, k, 0, 0], place(1, right)),
        ]

    def down(blk, k):
        return [
            copy(blk, k, 5, row_out.at[k, 0], row_halo.at[blk, k, 1], place(-1, lon)),
            copy(blk, k, 6, corner_out.at[k, 0, 0], corner_halo.at[blk, k, 1, 1], place(-1, left)),
            copy(blk, k, 7, corner_out.at[k, 0, 1], corner_halo.at[blk, k, 1, 0], place(-1, right)),
        ]

    def ring_copy(blk, k, step):
        return pltpu.make_async_remote_copy(
            src_ref=row_out.at[k, 1], dst_ref=ring[blk][k].at[core, chip],
            send_sem=ring_send.at[blk, k, step], recv_sem=ring_recv.at[blk, k, step],
            device_id=peer(step), device_id_type=MESH,
        )

    def forward(blk, k):
        return pltpu.make_async_remote_copy(
            src_ref=ring[blk][k].at[core], dst_ref=ring[blk][k].at[core],
            send_sem=ring_send.at[blk, k, 0], recv_sem=ring_recv.at[blk, k, 0],
            device_id=(sec, lat, sibling), device_id_type=MESH,
        )

    def send_edges(blk, k):
        for side, edge in enumerate((LOW, COL_HIGH)):
            for n, (b, big) in enumerate(edge):
                for a in range(2):
                    at = slice(big * NR, (big + 1) * NR)
                    col_out[k, side, n, a] = (
                        state[k, 2 * a + b, at, :] * share[2 * a + b, at, :]
                    ).astype(BF16)
        for side, edge in enumerate((LOW, ROW_HIGH)):
            for n, (a, big) in enumerate(edge):
                for b in range(2):
                    at = pl.ds(big, NT, stride=NR)
                    row_out[k, side, n, b] = (
                        state[k, 2 * a + b, at, :] * share[2 * a + b, at, :]
                    ).astype(BF16)
        tmp[9:16, :] = jnp.zeros((7, 128), F32)
        for rside, redge in enumerate((LOW, ROW_HIGH)):
            for cside, cedge in enumerate((LOW, COL_HIGH)):
                for n, (a, rbig) in enumerate(redge):
                    for m, (b, cbig) in enumerate(cedge):
                        at = slice(cbig * NR + rbig, cbig * NR + rbig + 1)
                        tmp[3 * n + m : 3 * n + m + 1, :] = (
                            state[k, 2 * a + b, at, :] * share[2 * a + b, at, :]
                        )
                corner_out[k, rside, cside] = tmp[0:16, :].astype(BF16)
        start(sideways(blk, k))
        pl.when(has_north)(lambda: start(up(blk, k)))
        pl.when(has_south)(lambda: start(down(blk, k)))

    def send_fold(blk, k):
        @pl.when(top)
        def _():
            start([ring_copy(blk, k, s) for s in (4, 3, 5, 2, 6, 1, 7)])
            ring[blk][k][core, chip] = row_out[k, 1]

    def edges_sent(blk, k):
        sent(sideways(blk, k))
        pl.when(has_north)(lambda: sent(up(blk, k)))
        pl.when(has_south)(lambda: sent(down(blk, k)))
        pl.when(top)(lambda: sent([ring_copy(blk, k, s) for s in range(1, 8)]))

    def build_taps(blk):
        taps[...] = jnp.zeros_like(taps)
        tmp[0:16, :] = jnp.zeros((16, 128), F32)
        low = lane_low((8, 128))
        for row in range(7):
            for k in range(3):
                for e in range(7):
                    tmp[1 + e : 2 + e, :] = kernel_taps[row, e, blk : blk + 1, k * 128 : (k + 1) * 128]
                now, before = tmp[1:9, :], tmp[0:8, :]
                at = slice(8 * (row + 1), 8 * (row + 2))
                taps[2 * k, at, :] = jnp.where(low, now, pltpu.roll(before, 64, 1))
                taps[2 * k + 1, at, :] = jnp.where(low, pltpu.roll(now, 64, 1), before)

    def build_weights(blk, k):
        slot = (3 * blk + k) % 2

        def weights(i, _):
            dr, dt = i // 4, lax.rem(i, 4)
            diag = (
                lax.broadcasted_iota(jnp.int32, (64, 128), 0)
                == lax.broadcasted_iota(jnp.int32, (64, 128), 1) % 64
            )
            for g in range(2):
                for pa in range(2):
                    for pb in range(2):
                        to = pl.ds(pl.multiple_of(dr * 256 + pa * 128 + pb * 64, 64), 64)
                        for r in range(2):
                            at = (2 * dr + pa + 1 - r) * 8 + 2 * dt + pb
                            value = jnp.where(diag, taps[2 * k + g, pl.ds(at, 1), :], 0.0)
                            rhs[slot, g, dt, to, r * 128 : (r + 1) * 128] = value.astype(BF16)
            return 0

        lax.fori_loop(0, 16, weights, 0)

    def conv_at(g, a, first, count, stride=None):
        return pl.ds((2 * g + a) * NM + first, count, stride=stride)

    def convolve(blk, k):
        slot = (3 * blk + k) % 2

        def own(i, _):
            for j in range(5):
                big = 5 * i + j
                src = pl.ds(pl.multiple_of(big * NR, NR), NR)
                for a in range(2):
                    for b in range(2):
                        value = state[k, 2 * a + b, src, :] * share[2 * a + b, src, :]
                        padded[2 * (1 - a) + 1 - b, pl.ds((big + 1 + b) * QR + 1 + a, NR), :] = value
            return 0

        lax.fori_loop(0, HALF // 5, own, 0)
        arrived(sideways(blk, k))
        pl.when(has_north)(lambda: arrived(down(blk, k)))
        pl.when(has_south)(lambda: arrived(up(blk, k)))
        for side, places in enumerate((LOW, ROW_TOP)):
            for n, (pa, pr) in enumerate(places):
                for b in range(2):
                    padded[2 * pa + 1 - b, pl.ds((1 + b) * QR + pr, NT, stride=QR), :] = row_halo[
                        blk, k, side, n, b
                    ].astype(F32)
        for side, places in enumerate((LOW, COL_TOP)):
            for n, (pb, pt) in enumerate(places):
                for a in range(2):
                    at = pt * QR + 1 + a
                    padded[2 * (1 - a) + pb, at : at + NR, :] = col_halo[blk, k, side, n, a].astype(F32)
        for rside, rplaces in enumerate((LOW, ROW_TOP)):
            for cside, cplaces in enumerate((LOW, COL_TOP)):
                tmp[0:16, :] = corner_halo[blk, k, rside, cside].astype(F32)
                for n, (pa, pr) in enumerate(rplaces):
                    for m, (pb, pt) in enumerate(cplaces):
                        at = pt * QR + pr
                        padded[2 * pa + pb, at : at + 1, :] = tmp[3 * n + m : 3 * n + m + 1, :]

        def pair_up(big, _):
            at = pl.ds(pl.multiple_of(big * 8 * QR, 8 * QR), 8 * QR)
            low = lane_low((8 * QR, 128))
            for pa in range(2):
                even, odd = padded[2 * pa, at, :], padded[2 * pa + 1, at, :]
                paired[0, pa, at, :] = jnp.where(low, even, pltpu.roll(odd, 64, 1))
                paired[1, pa, at, :] = jnp.where(low, pltpu.roll(even, 64, 1), odd)
            return 0

        lax.fori_loop(0, NT // 8, pair_up, 0)

        def spread(i, _):
            for j in range(4):
                big = 4 * i + j
                to = pl.ds(pl.multiple_of(big * NR, NR), NR)
                for g in range(2):
                    for d in range(4):
                        for pa in range(2):
                            c0 = d * 256 + pa * 128
                            lhs[g, to, c0 : c0 + 128] = paired[
                                g, pa, pl.ds(big * QR + d, NR), :
                            ].astype(BF16)
            return 0

        lax.fori_loop(0, NT // 4, spread, 0)
        for g in range(2):
            total = None
            for d in range(4):
                part = jnp.dot(
                    lhs[g, d * NR : d * NR + USED, :], rhs[slot, g, d], preferred_element_type=F32
                )
                total = part if total is None else total + part
            for a in range(2):
                table[k, conv_at(g, a, 0, USED), :] = total[:, a * 128 : (a + 1) * 128]

    def conv_rows(a, first, count, stride=None):
        low = lane_low((count, 128))
        chunks = []
        for k in range(3):
            even = table[k, conv_at(0, a, first, count, stride), :]
            odd = table[k, conv_at(1, a, first, count, stride), :]
            chunks.append(
                [
                    jnp.where(low, even, pltpu.roll(odd, 64, 1)),
                    jnp.where(low, pltpu.roll(even, 64, 1), odd),
                ]
            )
        return chunks

    def feed(blk, chunks):
        centre = jnp.sum(chunks[0] + chunks[1] + chunks[2], axis=1, keepdims=True) * (1.0 / CH)
        chunks = [c - centre for c in chunks]
        squares = chunks[0] * chunks[0] + chunks[1] * chunks[1] + chunks[2] * chunks[2]
        scale = lax.rsqrt(jnp.sum(squares, axis=1, keepdims=True) * (1.0 / CH) + 1e-06)
        normed = jnp.concatenate(
            [
                (c * scale * gain[blk : blk + 1, k * 128 : (k + 1) * 128]).astype(BF16)
                for k, c in enumerate(chunks)
            ],
            axis=1,
        )
        update = None
        for f in range(0, FF, PIECE):
            u = jnp.dot(normed, expand[:, f : f + PIECE], preferred_element_type=F32)
            h = 0.5 * u
            t = jnp.tanh(u * (0.7978845608028654 + 0.035677408136300125 * (u * u)))
            part = jnp.dot(
                (h + h * t).astype(BF16), contract[f : f + PIECE, :], preferred_element_type=F32
            )
            update = part if update is None else update + part
        return update

    def pass_on(blk, k):
        @pl.when(top)
        def _():
            for s in range(1, 8):
                ring_copy(blk, k, s).wait_recv()
            forward(blk, k).start()

    def fold_in(blk, k):
        @pl.when(top)
        def _():
            forward(blk, k).wait()
            first = lax.rem(fold[0] - 92 + NLON, NLON)
            sector = lax.div(first, COLS)
            off = first - sector * COLS
            at_out = lax.broadcasted_iota(jnp.int32, (2 * NT, 2 * NT), 0)
            at_in = lax.broadcasted_iota(jnp.int32, (2 * NT, 2 * NT), 1)
            wanted = off + 95 - jnp.where(at_out >= NT, 2 * (at_out - NT) + 1, 2 * at_out)
            pair = jnp.where(at_in >= NT, at_in - NT, at_in)
            column = 2 * pair + jnp.where(at_in >= NT, 1, 0)
            got = jnp.zeros((2 * NT, CH), F32)
            for s in range(3):
                source = lax.rem(sector + s, LONS)
                picked = jnp.where((column + s * COLS == wanted) & (pair < HALF), 1.0, 0.0).astype(BF16)
                strip = ring[blk][k][lax.rem(source, 2), lax.div(source, 2)]
                rows = [strip[2 - n].reshape(2 * NT, 128) for n in range(3)]
                got += jnp.dot(picked, jnp.concatenate(rows, axis=1), preferred_element_type=F32)
            low = lane_low((56, 128))
            for n in range(3):
                for pb in range(2):
                    at = (2 * n + pb) * 64
                    tmp[at : at + NT, :] = got[pb * NT : (pb + 1) * NT, n * 128 : (n + 1) * 128]
                    tmp[at + NT : at + 56, :] = jnp.zeros((8, 128), F32)
                    value = tmp[at : at + 56, :]
                    turned = pltpu.roll(value, 64, 1)
                    folded[0, n, pb] = jnp.where(low, value, turned)
                    folded[1, n, pb] = jnp.where(low, turned, value)
            for g in range(2):
                for i, (a, big) in enumerate(ROW_HIGH):
                    at = conv_at(g, a, big, NT, NR)
                    total = table[k, at, :]
                    for n in range(i + 1):
                        row = 8 * (7 + n - i)
                        for e in range(8):
                            total += (
                                folded[g, n, e % 2, e // 2 : e // 2 + NT, :]
                                * taps[2 * k + g, row + e : row + e + 1, :]
                            )
                    table[k, at, :] = total

    def mlp(blk):
        for c in mlp_loads(blk):
            c.wait()
        tile = 240
        for a in range(2):
            for i in range(USED // tile):
                at = slice(i * tile, (i + 1) * tile)
                update = feed(blk, [jnp.concatenate(c, axis=0) for c in conv_rows(a, i * tile, tile)])
                for b in range(2):
                    for k in range(3):
                        state[k, 2 * a + b, at, :] += (
                            share[2 * a + b, at, :]
                            * update[b * tile : (b + 1) * tile, k * 128 : (k + 1) * 128]
                        )

    def remap(k):
        for side in range(2):
            flux_copy(k, 1 - side).wait_recv()

            def widened(i, _, side=side):
                at = pl.multiple_of(i * 288, 288)
                table[k, pl.ds(3 * side * CELLS + at, 288), :] = incoming[
                    k, side, pl.ds(at, 288), :
                ].astype(F32)
                return 0

            lax.fori_loop(0, CELLS // 288, widened, 0)

        def gather_cells(big, _):
            base = pl.multiple_of(big * NR, NR)
            for a in range(2):
                for b in range(2):
                    for r in range(NR):
                        paired[a, b, pl.ds(base + r, 1), :] = table[
                            k, pl.ds(picks[2 * r + a, 2 * big + b], 1), :
                        ]
            return 0

        lax.fori_loop(0, HALF, gather_cells, 0)
        for a in range(2):
            for b in range(2):
                state[k, 2 * a + b, 0:USED, :] += paired[a, b, 0:USED, :]

    build_taps(0)
    build_weights(0, 0)
    build_weights(0, 1)
    remap(0)
    send_edges(0, 0)
    for side in range(2):
        flux_copy(2, side).start()
    send_fold(0, 0)
    remap(1)
    send_edges(0, 1)
    send_fold(0, 1)
    convolve(0, 0)
    build_weights(0, 2)
    remap(2)
    send_edges(0, 2)
    send_fold(0, 2)
    convolve(0, 1)
    pass_on(0, 0)
    pass_on(0, 1)
    convolve(0, 2)
    pass_on(0, 2)
    for k in range(3):
        fold_in(0, k)
    mlp(0)
    start(mlp_loads(1))
    for k in range(3):
        edges_sent(0, k)
        send_edges(1, k)
    for k in range(3):
        send_fold(1, k)
    build_taps(1)
    build_weights(1, 0)
    build_weights(1, 1)
    convolve(1, 0)
    build_weights(1, 2)
    convolve(1, 1)
    pass_on(1, 0)
    pass_on(1, 1)
    convolve(1, 2)
    pass_on(1, 2)
    for k in range(3):
        fold_in(1, k)
    mlp(1)

    def natural(i, _):
        for j in range(3):
            big = 3 * i + j
            at = pl.ds(pl.multiple_of(big * NR, NR), NR)
            for b in range(2):
                for k in range(3):
                    own = ((j * 2 + b) * 3 + k) * ROWS
                    for a in range(2):
                        tmp[pl.ds(own + a, NR, stride=2), :] = state[k, 2 * a + b, at, :]
                    out[2 * big + b, :, k * 128 : (k + 1) * 128] = tmp[own : own + ROWS, :].astype(BF16)
        return 0

    lax.fori_loop(0, HALF // 3, natural, 0)
    for k in range(3):
        edges_sent(1, k)
        for side in range(2):
            flux_copy(k, side).wait_send()


def step(picks, sea_mask, fold, weight, taps, gain, atmos, ocean, expand, contract):
    vmem, smem = (pl.BlockSpec(memory_space=m) for m in (pltpu.VMEM, pltpu.SMEM))
    anywhere = pl.BlockSpec(memory_space=pl.ANY)
    edges = [(3, 2, 3, 2, NT, 128), (3, 2, 3, 2, NR, 128), (3, 2, 2, 16, 128)]
    return pl.pallas_call(
        ocean_kernel,
        out_shape=jax.ShapeDtypeStruct((COLS, ROWS, CH), BF16),
        in_specs=[smem] * 3 + [vmem] * 3 + [anywhere] * 4,
        out_specs=vmem,
        scratch_shapes=[
            pltpu.VMEM((2 * CELLS, CA), BF16),
            pltpu.VMEM((COLS, ROWS, CH), BF16),
            pltpu.VMEM((3, 4 * CELLS + 8, 128), F32),
            pltpu.VMEM((3, 2, CELLS, 128), BF16),
            pltpu.VMEM((3, 2, CELLS, 128), BF16),
            pltpu.VMEM((3, 4, NM, 128), F32),
            pltpu.VMEM((4, NM, 128), F32),
            *(pltpu.VMEM(e, BF16) for e in edges),
            *(pltpu.VMEM((2, *e), BF16) for e in edges),
            *(pltpu.VMEM((2, LONS // 2, 3, 2, NT, 128), BF16) for _ in range(6)),
            pltpu.VMEM((4, QR * QT, 128), F32),
            pltpu.VMEM((2, 2, QR * NT, 128), F32),
            pltpu.VMEM((2, NT * NR, 1024), BF16),
            pltpu.VMEM((2, 2, 4, 1024, 256), BF16),
            pltpu.VMEM((18 * ROWS, 128), F32),
            pltpu.VMEM((6, 72, 128), F32),
            pltpu.VMEM((2, 3, 2, 56, 128), F32),
            pltpu.VMEM((CH, FF), BF16),
            pltpu.VMEM((FF, CH), BF16),
            pltpu.SemaphoreType.DMA((5,)),
            pltpu.SemaphoreType.DMA((3, 2)),
            pltpu.SemaphoreType.DMA((3, 2)),
            pltpu.SemaphoreType.DMA((2, 3, 8)),
            pltpu.SemaphoreType.DMA((2, 3, 8)),
            pltpu.SemaphoreType.DMA((2, 3, 8)),
            pltpu.SemaphoreType.DMA((2, 3, 8)),
        ],
        compiler_params=pltpu.CompilerParams(
            collective_id=0, has_side_effects=True, vmem_limit_bytes=VLIMIT
        ),
    )(picks, sea_mask, fold, weight, taps, gain, atmos, ocean, expand, contract)


def body(atmos, ocean, remap, fold, sea_mask, flux_weight, dw_kernel, norm_gain, w_in, w_out):
    band = lax.axis_index(("sec", "lat"))
    lon = lax.axis_index("lon")
    row = remap // NLON
    col = (remap - row * NLON - lon * COLS + HALF + NLON) % NLON
    picks = jnp.where(sea_mask == 0, 4 * CELLS, col * ROWS + row - band * ROWS)
    atmos = atmos.transpose(1, 0, 2).reshape(COLS * ROWS, CA)
    ocean = ocean.transpose(1, 0, 2)
    taps = dw_kernel.transpose(1, 2, 0, 3)
    out = step(picks, sea_mask, fold, flux_weight, taps, norm_gain, atmos, ocean, w_in, w_out)
    return out.transpose(1, 0, 2)


def solution(mesh):
    return jax.shard_map(
        body,
        mesh=mesh,
        in_specs=(
            P(("sec", "lat"), "lon", None),
            P(("sec", "lat"), "lon", None),
            P(("sec", "lat"), "lon"),
            P("lon"),
            P(("sec", "lat"), "lon"),
            P(),
            P(),
            P(),
            P(),
            P(),
        ),
        out_specs=P(("sec", "lat"), "lon", None),
        check_vma=False,
    )
```

```python
import jax
import jax.numpy as jnp
from jax import lax
from jax.experimental import pallas as pl
from jax.experimental.pallas import tpu as pltpu
from jax.sharding import PartitionSpec as P

ROWS, COLS, CH, CA, FF = 32, 90, 384, 512, 1536
HALF = 45
CELLS = ROWS * HALF
BANDS, LONS = 8, 16
NLON = COLS * LONS
NR, NT, NM, USED = 16, 48, 768, 720
QR, QT = 24, 50
LOW = ((0, 0), (1, 0), (0, 1))
ROW_HIGH = ((1, 14), (0, 15), (1, 15))
COL_HIGH = ((1, 43), (0, 44), (1, 44))
ROW_TOP = ((1, 17), (0, 18), (1, 18))
COL_TOP = ((1, 46), (0, 47), (1, 47))
MESH = pl.DeviceIdType.MESH
F32, BF16 = jnp.float32, jnp.bfloat16
VLIMIT = 60 * 2**20
PIECE = 1536


def lane_low(shape):
    return lax.broadcasted_iota(jnp.int32, shape, len(shape) - 1) < 64


def ocean_kernel(
    picks, sea, fold, weight, kernel_taps, gain, atmos_in, ocean_in, expand_all, contract_all,
    out,
    atmos, ocean, table, outgoing, incoming, state, share, row_out, col_out, corner_out, row_halo, col_halo, corner_halo,
    ring_00, ring_01, ring_02, ring_10, ring_11, ring_12, padded, paired, lhs, rhs, tmp, taps, folded, saved, expand, contract,
    load_sem, flux_send, flux_recv, halo_send, halo_recv, ring_send, ring_recv,
):
    ring = ((ring_00, ring_01, ring_02), (ring_10, ring_11, ring_12))

    def load(n, src, dst):
        return pltpu.make_async_copy(src, dst, load_sem.at[n])

    atmos_loads = [
        load(side, atmos_in.at[pl.ds(side * CELLS, CELLS)], atmos.at[pl.ds(side * CELLS, CELLS)])
        for side in range(2)
    ]
    ocean_load = load(2, ocean_in, ocean)

    def mlp_loads(blk):
        return [load(3, expand_all.at[blk], expand), load(4, contract_all.at[blk], contract)]

    def start(copies):
        for c in copies:
            c.start()

    def arrived(copies):
        for c in copies:
            c.wait_recv()

    def sent(copies):
        for c in copies:
            c.wait_send()

    start(atmos_loads)
    ocean_load.start()
    start(mlp_loads(0))

    sec, lat, lon = (lax.axis_index(n) for n in ("sec", "lat", "lon"))
    band = sec * 4 + lat
    chip, core = lon // 2, lax.rem(lon, 2)
    sibling = lon + 1 - 2 * core
    left, right = lax.rem(lon + LONS - 1, LONS), lax.rem(lon + 1, LONS)
    has_north, has_south, top = band < BANDS - 1, band > 0, band == BANDS - 1

    def place(step, where):
        other = band + step
        return (other // 4, lax.rem(other, 4), where)

    def peer(step):
        return (sec, lat, lax.rem(lon + 2 * step, LONS))

    barrier = pltpu.get_barrier_semaphore()

    def greet(device):
        pl.semaphore_signal(barrier, inc=1, device_id=device, device_id_type=MESH)

    greet((sec, lat, left))
    greet((sec, lat, right))
    pl.when(has_north)(lambda: [greet(place(1, w)) for w in (left, lon, right)] and None)
    pl.when(has_south)(lambda: [greet(place(-1, w)) for w in (left, lon, right)] and None)
    pl.when(top)(lambda: [greet(peer(s)) for s in range(1, 8)] and None)
    greeted = 2 + jnp.where(has_north, 3, 0) + jnp.where(has_south, 3, 0) + jnp.where(top, 7, 0)
    pl.semaphore_wait(barrier, greeted)

    def flux_copy(k, side):
        return pltpu.make_async_remote_copy(
            src_ref=outgoing.at[k, side], dst_ref=incoming.at[k, 1 - side],
            send_sem=flux_send.at[k, side], recv_sem=flux_recv.at[k, 1 - side],
            device_id=(sec, lat, (left, right)[side]), device_id_type=MESH,
        )

    for k in range(3):
        for side in range(2):
            if k == 0:
                atmos_loads[side].wait()

            def cells(i, _, k=k, side=side):
                at = pl.multiple_of(i * 288, 288)
                value = jnp.dot(
                    atmos[pl.ds(side * CELLS + at, 288), :],
                    weight[:, k * 128 : (k + 1) * 128],
                    preferred_element_type=F32,
                ).astype(BF16)
                outgoing[k, side, pl.ds(at, 288), :] = value
                table[k, pl.ds((1 + side) * CELLS + at, 288), :] = value.astype(F32)
                return 0

            lax.fori_loop(0, CELLS // 288, cells, 0)
            if k < 2:
                flux_copy(k, side).start()
        table[k, 4 * CELLS : 4 * CELLS + 8, :] = jnp.zeros((8, 128), F32)

    for q in range(4):
        share[q, USED:NM, :] = jnp.zeros((NM - USED, 128), F32)
        for k in range(3):
            state[k, q, USED:NM, :] = jnp.zeros((NM - USED, 128), F32)
    tmp[0:16, :] = jnp.zeros((16, 128), F32)
    tmp[1:2, :] = jnp.ones((1, 128), F32)

    def share_cells(big, _):
        base = pl.multiple_of(big * NR, NR)
        for a in range(2):
            for b in range(2):
                for r in range(NR):
                    share[2 * a + b, pl.ds(base + r, 1), :] = tmp[
                        pl.ds(sea[2 * r + a, 2 * big + b], 1), :
                    ]
        return 0

    lax.fori_loop(0, HALF, share_cells, 0)
    ocean_load.wait()

    def ocean_cells(big, _):
        at = pl.ds(pl.multiple_of(big * NR, NR), NR)
        for b in range(2):
            for k in range(3):
                own = (3 * b + k) * ROWS
                tmp[own : own + ROWS, :] = ocean[2 * big + b, :, k * 128 : (k + 1) * 128].astype(F32)
                for a in range(2):
                    state[k, 2 * a + b, at, :] = tmp[pl.ds(own + a, NR, stride=2), :]
        return 0

    lax.fori_loop(0, HALF, ocean_cells, 0)
    padded[...] = jnp.zeros_like(padded)

    @pl.when(jnp.logical_not(has_south))
    def _():
        for blk in range(2):
            row_halo[blk, :, 0] = jnp.zeros((3, *row_halo.shape[3:]), BF16)
            corner_halo[blk, :, 0] = jnp.zeros((3, *corner_halo.shape[3:]), BF16)

    @pl.when(top)
    def _():
        for blk in range(2):
            row_halo[blk, :, 1] = jnp.zeros((3, *row_halo.shape[3:]), BF16)
            corner_halo[blk, :, 1] = jnp.zeros((3, *corner_halo.shape[3:]), BF16)

    def copy(blk, k, n, src, dst, device):
        return pltpu.make_async_remote_copy(
            src_ref=src, dst_ref=dst, send_sem=halo_send.at[blk, k, n], recv_sem=halo_recv.at[blk, k, n],
            device_id=device, device_id_type=MESH,
        )

    def sideways(blk, k):
        return [
            copy(blk, k, 0, col_out.at[k, 1], col_halo.at[blk, k, 0], (sec, lat, right)),
            copy(blk, k, 1, col_out.at[k, 0], col_halo.at[blk, k, 1], (sec, lat, left)),
        ]

    def up(blk, k):
        return [
            copy(blk, k, 2, row_out.at[k, 1], row_halo.at[blk, k, 0], place(1, lon)),
            copy(blk, k, 3, corner_out.at[k, 1, 0], corner_halo.at[blk, k, 0, 1], place(1, left)),
            copy(blk, k, 4, corner_out.at[k, 1, 1], corner_halo.at[blk, k, 0, 0], place(1, right)),
        ]

    def down(blk, k):
        return [
            copy(blk, k, 5, row_out.at[k, 0], row_halo.at[blk, k, 1], place(-1, lon)),
            copy(blk, k, 6, corner_out.at[k, 0, 0], corner_halo.at[blk, k, 1, 1], place(-1, left)),
            copy(blk, k, 7, corner_out.at[k, 0, 1], corner_halo.at[blk, k, 1, 0], place(-1, right)),
        ]

    def ring_copy(blk, k, step):
        return pltpu.make_async_remote_copy(
            src_ref=row_out.at[k, 1], dst_ref=ring[blk][k].at[core, chip],
            send_sem=ring_send.at[blk, k, step], recv_sem=ring_recv.at[blk, k, step],
            device_id=peer(step), device_id_type=MESH,
        )

    def forward(blk, k):
        return pltpu.make_async_remote_copy(
            src_ref=ring[blk][k].at[core], dst_ref=ring[blk][k].at[core],
            send_sem=ring_send.at[blk, k, 0], recv_sem=ring_recv.at[blk, k, 0],
            device_id=(sec, lat, sibling), device_id_type=MESH,
        )

    def send_edges(blk, k):
        for side, edge in enumerate((LOW, COL_HIGH)):
            for n, (b, big) in enumerate(edge):
                for a in range(2):
                    at = slice(big * NR, (big + 1) * NR)
                    col_out[k, side, n, a] = (
                        state[k, 2 * a + b, at, :] * share[2 * a + b, at, :]
                    ).astype(BF16)
        for side, edge in enumerate((LOW, ROW_HIGH)):
            for n, (a, big) in enumerate(edge):
                for b in range(2):
                    at = pl.ds(big, NT, stride=NR)
                    row_out[k, side, n, b] = (
                        state[k, 2 * a + b, at, :] * share[2 * a + b, at, :]
                    ).astype(BF16)
        tmp[9:16, :] = jnp.zeros((7, 128), F32)
        for rside, redge in enumerate((LOW, ROW_HIGH)):
            for cside, cedge in enumerate((LOW, COL_HIGH)):
                for n, (a, rbig) in enumerate(redge):
                    for m, (b, cbig) in enumerate(cedge):
                        at = slice(cbig * NR + rbig, cbig * NR + rbig + 1)
                        tmp[3 * n + m : 3 * n + m + 1, :] = (
                            state[k, 2 * a + b, at, :] * share[2 * a + b, at, :]
                        )
                corner_out[k, rside, cside] = tmp[0:16, :].astype(BF16)
        start(sideways(blk, k))
        pl.when(has_north)(lambda: start(up(blk, k)))
        pl.when(has_south)(lambda: start(down(blk, k)))

    def send_fold(blk, k):
        @pl.when(top)
        def _():
            start([ring_copy(blk, k, s) for s in (4, 3, 5, 2, 6, 1, 7)])
            ring[blk][k][core, chip] = row_out[k, 1]

    def edges_sent(blk, k):
        sent(sideways(blk, k))
        pl.when(has_north)(lambda: sent(up(blk, k)))
        pl.when(has_south)(lambda: sent(down(blk, k)))
        pl.when(top)(lambda: sent([ring_copy(blk, k, s) for s in range(1, 8)]))

    def build_taps(blk):
        taps[...] = jnp.zeros_like(taps)
        tmp[0:16, :] = jnp.zeros((16, 128), F32)
        low = lane_low((8, 128))
        for row in range(7):
            for k in range(3):
                for e in range(7):
                    tmp[1 + e : 2 + e, :] = kernel_taps[row, e, blk : blk + 1, k * 128 : (k + 1) * 128]
                now, before = tmp[1:9, :], tmp[0:8, :]
                at = slice(8 * (row + 1), 8 * (row + 2))
                taps[2 * k, at, :] = jnp.where(low, now, pltpu.roll(before, 64, 1))
                taps[2 * k + 1, at, :] = jnp.where(low, pltpu.roll(now, 64, 1), before)

    def build_weights(blk, k):
        slot = (3 * blk + k) % 2

        def weights(i, _):
            dr, dt = i // 4, lax.rem(i, 4)
            diag = (
                lax.broadcasted_iota(jnp.int32, (64, 128), 0)
                == lax.broadcasted_iota(jnp.int32, (64, 128), 1) % 64
            )
            for g in range(2):
                for pa in range(2):
                    for pb in range(2):
                        to = pl.ds(pl.multiple_of(dr * 256 + pa * 128 + pb * 64, 64), 64)
                        for r in range(2):
                            at = (2 * dr + pa + 1 - r) * 8 + 2 * dt + pb
                            value = jnp.where(diag, taps[2 * k + g, pl.ds(at, 1), :], 0.0)
                            rhs[slot, g, dt, to, r * 128 : (r + 1) * 128] = value.astype(BF16)
            return 0

        lax.fori_loop(0, 16, weights, 0)

    def conv_at(g, a, first, count, stride=None):
        return pl.ds((2 * g + a) * NM + first, count, stride=stride)

    def convolve(blk, k):
        slot = (3 * blk + k) % 2

        def own(i, _):
            for j in range(5):
                big = 5 * i + j
                src = pl.ds(pl.multiple_of(big * NR, NR), NR)
                for a in range(2):
                    for b in range(2):
                        value = state[k, 2 * a + b, src, :] * share[2 * a + b, src, :]
                        padded[2 * (1 - a) + 1 - b, pl.ds((big + 1 + b) * QR + 1 + a, NR), :] = value
            return 0

        lax.fori_loop(0, HALF // 5, own, 0)
        arrived(sideways(blk, k))
        pl.when(has_north)(lambda: arrived(down(blk, k)))
        pl.when(has_south)(lambda: arrived(up(blk, k)))
        for side, places in enumerate((LOW, ROW_TOP)):
            for n, (pa, pr) in enumerate(places):
                for b in range(2):
                    padded[2 * pa + 1 - b, pl.ds((1 + b) * QR + pr, NT, stride=QR), :] = row_halo[
                        blk, k, side, n, b
                    ].astype(F32)
        for side, places in enumerate((LOW, COL_TOP)):
            for n, (pb, pt) in enumerate(places):
                for a in range(2):
                    at = pt * QR + 1 + a
                    padded[2 * (1 - a) + pb, at : at + NR, :] = col_halo[blk, k, side, n, a].astype(F32)
        for rside, rplaces in enumerate((LOW, ROW_TOP)):
            for cside, cplaces in enumerate((LOW, COL_TOP)):
                tmp[0:16, :] = corner_halo[blk, k, rside, cside].astype(F32)
                for n, (pa, pr) in enumerate(rplaces):
                    for m, (pb, pt) in enumerate(cplaces):
                        at = pt * QR + pr
                        padded[2 * pa + pb, at : at + 1, :] = tmp[3 * n + m : 3 * n + m + 1, :]

        def pair_up(big, _):
            at = pl.ds(pl.multiple_of(big * 8 * QR, 8 * QR), 8 * QR)
            low = lane_low((8 * QR, 128))
            for pa in range(2):
                even, odd = padded[2 * pa, at, :], padded[2 * pa + 1, at, :]
                paired[0, pa, at, :] = jnp.where(low, even, pltpu.roll(odd, 64, 1))
                paired[1, pa, at, :] = jnp.where(low, pltpu.roll(even, 64, 1), odd)
            return 0

        lax.fori_loop(0, NT // 8, pair_up, 0)

        def spread(i, _):
            for j in range(4):
                big = 4 * i + j
                to = pl.ds(pl.multiple_of(big * NR, NR), NR)
                for g in range(2):
                    for d in range(4):
                        for pa in range(2):
                            c0 = d * 256 + pa * 128
                            lhs[g, to, c0 : c0 + 128] = paired[
                                g, pa, pl.ds(big * QR + d, NR), :
                            ].astype(BF16)
            return 0

        lax.fori_loop(0, NT // 4, spread, 0)
        for g in range(2):
            total = None
            for d in range(4):
                part = jnp.dot(
                    lhs[g, d * NR : d * NR + USED, :], rhs[slot, g, d], preferred_element_type=F32
                )
                total = part if total is None else total + part
            for a in range(2):
                table[k, conv_at(g, a, 0, USED), :] = total[:, a * 128 : (a + 1) * 128]

    def conv_rows(a, first, count, stride=None):
        low = lane_low((count, 128))
        chunks = []
        for k in range(3):
            even = table[k, conv_at(0, a, first, count, stride), :]
            odd = table[k, conv_at(1, a, first, count, stride), :]
            chunks.append(
                [
                    jnp.where(low, even, pltpu.roll(odd, 64, 1)),
                    jnp.where(low, pltpu.roll(even, 64, 1), odd),
                ]
            )
        return chunks

    def feed(blk, chunks):
        centre = jnp.sum(chunks[0] + chunks[1] + chunks[2], axis=1, keepdims=True) * (1.0 / CH)
        chunks = [c - centre for c in chunks]
        squares = chunks[0] * chunks[0] + chunks[1] * chunks[1] + chunks[2] * chunks[2]
        scale = lax.rsqrt(jnp.sum(squares, axis=1, keepdims=True) * (1.0 / CH) + 1e-06)
        normed = jnp.concatenate(
            [
                (c * scale * gain[blk : blk + 1, k * 128 : (k + 1) * 128]).astype(BF16)
                for k, c in enumerate(chunks)
            ],
            axis=1,
        )
        update = None
        for f in range(0, FF, PIECE):
            u = jnp.dot(normed, expand[:, f : f + PIECE], preferred_element_type=F32)
            h = 0.5 * u
            t = jnp.tanh(u * (0.7978845608028654 + 0.035677408136300125 * (u * u)))
            part = jnp.dot(
                (h + h * t).astype(BF16), contract[f : f + PIECE, :], preferred_element_type=F32
            )
            update = part if update is None else update + part
        return update

    def pass_on(blk, k):
        @pl.when(top)
        def _():
            for s in range(1, 8):
                ring_copy(blk, k, s).wait_recv()
            forward(blk, k).start()

    def fold_in(blk, k):
        @pl.when(top)
        def _():
            forward(blk, k).wait()
            first = lax.rem(fold[0] - 92 + NLON, NLON)
            sector = lax.div(first, COLS)
            off = first - sector * COLS
            at_out = lax.broadcasted_iota(jnp.int32, (2 * NT, 2 * NT), 0)
            at_in = lax.broadcasted_iota(jnp.int32, (2 * NT, 2 * NT), 1)
            wanted = off + 95 - jnp.where(at_out >= NT, 2 * (at_out - NT) + 1, 2 * at_out)
            pair = jnp.where(at_in >= NT, at_in - NT, at_in)
            column = 2 * pair + jnp.where(at_in >= NT, 1, 0)
            got = jnp.zeros((2 * NT, CH), F32)
            for s in range(3):
                source = lax.rem(sector + s, LONS)
                picked = jnp.where((column + s * COLS == wanted) & (pair < HALF), 1.0, 0.0).astype(BF16)
                strip = ring[blk][k][lax.rem(source, 2), lax.div(source, 2)]
                rows = [strip[2 - n].reshape(2 * NT, 128) for n in range(3)]
                got += jnp.dot(picked, jnp.concatenate(rows, axis=1), preferred_element_type=F32)
            low = lane_low((56, 128))
            for n in range(3):
                for pb in range(2):
                    at = (2 * n + pb) * 64
                    tmp[at : at + NT, :] = got[pb * NT : (pb + 1) * NT, n * 128 : (n + 1) * 128]
                    tmp[at + NT : at + 56, :] = jnp.zeros((8, 128), F32)
                    value = tmp[at : at + 56, :]
                    turned = pltpu.roll(value, 64, 1)
                    folded[0, n, pb] = jnp.where(low, value, turned)
                    folded[1, n, pb] = jnp.where(low, turned, value)
            for g in range(2):
                for i, (a, big) in enumerate(ROW_HIGH):
                    at = conv_at(g, a, big, NT, NR)
                    total = table[k, at, :]
                    for n in range(i + 1):
                        row = 8 * (7 + n - i)
                        for e in range(8):
                            total += (
                                folded[g, n, e % 2, e // 2 : e // 2 + NT, :]
                                * taps[2 * k + g, row + e : row + e + 1, :]
                            )
                    table[k, at, :] = total

    def mlp(blk):
        for c in mlp_loads(blk):
            c.wait()
        tile = 240
        row_30 = pl.ds(15, NT, stride=NR)

        def run(a, i):
            at = slice(i * tile, (i + 1) * tile)
            update = feed(blk, [jnp.concatenate(c, axis=0) for c in conv_rows(a, i * tile, tile)])
            for b in range(2):
                for k in range(3):
                    state[k, 2 * a + b, at, :] += (
                        share[2 * a + b, at, :]
                        * update[b * tile : (b + 1) * tile, k * 128 : (k + 1) * 128]
                    )

        @pl.when(top)
        def _():
            for k in range(3):
                for b in range(2):
                    saved[k, b] = state[k, b, row_30, :]

        run(0, 0)
        run(0, 1)
        pass_on(blk, 2)
        run(0, 2)
        for k in range(3):
            fold_in(blk, k)
        for i in range(USED // tile):
            run(1, i)

        @pl.when(top)
        def _():
            update = feed(blk, [jnp.concatenate(c, axis=0) for c in conv_rows(0, 15, NT, NR)])
            for b in range(2):
                for k in range(3):
                    state[k, b, row_30, :] = (
                        saved[k, b]
                        + share[b, row_30, :]
                        * update[b * NT : (b + 1) * NT, k * 128 : (k + 1) * 128]
                    )

    def remap(k):
        for side in range(2):
            flux_copy(k, 1 - side).wait_recv()

            def widened(i, _, side=side):
                at = pl.multiple_of(i * 288, 288)
                table[k, pl.ds(3 * side * CELLS + at, 288), :] = incoming[
                    k, side, pl.ds(at, 288), :
                ].astype(F32)
                return 0

            lax.fori_loop(0, CELLS // 288, widened, 0)

        def gather_cells(big, _):
            base = pl.multiple_of(big * NR, NR)
            for a in range(2):
                for b in range(2):
                    for r in range(NR):
                        paired[a, b, pl.ds(base + r, 1), :] = table[
                            k, pl.ds(picks[2 * r + a, 2 * big + b], 1), :
                        ]
            return 0

        lax.fori_loop(0, HALF, gather_cells, 0)
        for a in range(2):
            for b in range(2):
                state[k, 2 * a + b, 0:USED, :] += paired[a, b, 0:USED, :]

    build_taps(0)
    build_weights(0, 0)
    build_weights(0, 1)
    remap(0)
    send_edges(0, 0)
    for side in range(2):
        flux_copy(2, side).start()
    send_fold(0, 0)
    remap(1)
    send_edges(0, 1)
    send_fold(0, 1)
    convolve(0, 0)
    build_weights(0, 2)
    remap(2)
    send_edges(0, 2)
    send_fold(0, 2)
    convolve(0, 1)
    pass_on(0, 0)
    convolve(0, 2)
    pass_on(0, 1)
    mlp(0)
    start(mlp_loads(1))
    for k in range(3):
        edges_sent(0, k)
        send_edges(1, k)
    for k in range(3):
        send_fold(1, k)
    build_taps(1)
    build_weights(1, 0)
    build_weights(1, 1)
    convolve(1, 0)
    build_weights(1, 2)
    convolve(1, 1)
    pass_on(1, 0)
    convolve(1, 2)
    pass_on(1, 1)
    mlp(1)

    def natural(i, _):
        for j in range(3):
            big = 3 * i + j
            at = pl.ds(pl.multiple_of(big * NR, NR), NR)
            for b in range(2):
                for k in range(3):
                    own = ((j * 2 + b) * 3 + k) * ROWS
                    for a in range(2):
                        tmp[pl.ds(own + a, NR, stride=2), :] = state[k, 2 * a + b, at, :]
                    out[2 * big + b, :, k * 128 : (k + 1) * 128] = tmp[own : own + ROWS, :].astype(BF16)
        return 0

    lax.fori_loop(0, HALF // 3, natural, 0)
    for k in range(3):
        edges_sent(1, k)
        for side in range(2):
            flux_copy(k, side).wait_send()


def step(picks, sea_mask, fold, weight, taps, gain, atmos, ocean, expand, contract):
    vmem, smem = (pl.BlockSpec(memory_space=m) for m in (pltpu.VMEM, pltpu.SMEM))
    anywhere = pl.BlockSpec(memory_space=pl.ANY)
    edges = [(3, 2, 3, 2, NT, 128), (3, 2, 3, 2, NR, 128), (3, 2, 2, 16, 128)]
    return pl.pallas_call(
        ocean_kernel,
        out_shape=jax.ShapeDtypeStruct((COLS, ROWS, CH), BF16),
        in_specs=[smem] * 3 + [vmem] * 3 + [anywhere] * 4,
        out_specs=vmem,
        scratch_shapes=[
            pltpu.VMEM((2 * CELLS, CA), BF16),
            pltpu.VMEM((COLS, ROWS, CH), BF16),
            pltpu.VMEM((3, 4 * CELLS + 8, 128), F32),
            pltpu.VMEM((3, 2, CELLS, 128), BF16),
            pltpu.VMEM((3, 2, CELLS, 128), BF16),
            pltpu.VMEM((3, 4, NM, 128), F32),
            pltpu.VMEM((4, NM, 128), F32),
            *(pltpu.VMEM(e, BF16) for e in edges),
            *(pltpu.VMEM((2, *e), BF16) for e in edges),
            *(pltpu.VMEM((2, LONS // 2, 3, 2, NT, 128), BF16) for _ in range(6)),
            pltpu.VMEM((4, QR * QT, 128), F32),
            pltpu.VMEM((2, 2, QR * NT, 128), F32),
            pltpu.VMEM((2, NT * NR, 1024), BF16),
            pltpu.VMEM((2, 2, 4, 1024, 256), BF16),
            pltpu.VMEM((18 * ROWS, 128), F32),
            pltpu.VMEM((6, 72, 128), F32),
            pltpu.VMEM((2, 3, 2, 56, 128), F32),
            pltpu.VMEM((3, 2, NT, 128), F32),
            pltpu.VMEM((CH, FF), BF16),
            pltpu.VMEM((FF, CH), BF16),
            pltpu.SemaphoreType.DMA((5,)),
            pltpu.SemaphoreType.DMA((3, 2)),
            pltpu.SemaphoreType.DMA((3, 2)),
            pltpu.SemaphoreType.DMA((2, 3, 8)),
            pltpu.SemaphoreType.DMA((2, 3, 8)),
            pltpu.SemaphoreType.DMA((2, 3, 8)),
            pltpu.SemaphoreType.DMA((2, 3, 8)),
        ],
        compiler_params=pltpu.CompilerParams(
            collective_id=0, has_side_effects=True, vmem_limit_bytes=VLIMIT
        ),
    )(picks, sea_mask, fold, weight, taps, gain, atmos, ocean, expand, contract)


def body(atmos, ocean, remap, fold, sea_mask, flux_weight, dw_kernel, norm_gain, w_in, w_out):
    band = lax.axis_index(("sec", "lat"))
    lon = lax.axis_index("lon")
    row = remap // NLON
    col = (remap - row * NLON - lon * COLS + HALF + NLON) % NLON
    picks = jnp.where(sea_mask == 0, 4 * CELLS, col * ROWS + row - band * ROWS)
    atmos = atmos.transpose(1, 0, 2).reshape(COLS * ROWS, CA)
    ocean = ocean.transpose(1, 0, 2)
    taps = dw_kernel.transpose(1, 2, 0, 3)
    out = step(picks, sea_mask, fold, flux_weight, taps, norm_gain, atmos, ocean, w_in, w_out)
    return out.transpose(1, 0, 2)


def solution(mesh):
    return jax.shard_map(
        body,
        mesh=mesh,
        in_specs=(
            P(("sec", "lat"), "lon", None),
            P(("sec", "lat"), "lon", None),
            P(("sec", "lat"), "lon"),
            P("lon"),
            P(("sec", "lat"), "lon"),
            P(),
            P(),
            P(),
            P(),
            P(),
        ),
        out_specs=P(("sec", "lat"), "lon", None),
        check_vma=False,
    )
```
